32 devices in a mesh: rep: 4 (over y, x), blk: 2 (over core), tp: 4 (over z).
Axes of the slice: x: 2, y: 2, z: 4, core: 2. Of those that a mesh axis runs over, the one named last changes fastest.
Arguments:
- hidden: bfloat16 [16, 2048], P('rep', 'blk'), may hold values from -64 to 64
- ln_gain: float32 [2, 2048], P(None, 'blk'), may hold values from 0.1 to 1.9
- w_qkv: bfloat16 [2, 2048, 3, 2048], P(None, 'blk', None, 'tp'), may hold values from -0.125 to 0.125
- w_fc1: bfloat16 [2, 2048, 8192], P(None, 'blk', 'tp'), may hold values from -0.125 to 0.125
- w_out: bfloat16 [2, 2048, 2048], P(None, 'tp', 'blk'), may hold values from -0.125 to 0.125
- w_fc2: bfloat16 [2, 8192, 2048], P(None, 'tp', 'blk'), may hold values from -0.0625 to 0.0625
- caches: bfloat16 [2, 2, 64, 32, 2048], P(None, None, ('rep', 'blk'), None, 'tp'), may hold values from -110 to 110
- page_owner: int32 [64], P(('rep', 'blk')), may hold values from 0 to 15, as said below
- page_used: int32 [64], P(('rep', 'blk')), may hold values from 0 to 1, as said below
- page_fill: int32 [64], P(('rep', 'blk')), may hold values from 0 to 32, as said below
- page_tail: int32 [64], P(('rep', 'blk')), may hold values from 0 to 1
- positions: int32 [16], P('rep'), may hold values from 0 to 4095
Outputs:
- hidden_out: bfloat16 [16, 2048], P('rep', 'blk')
- caches_out: bfloat16 [2, 2, 64, 32, 2048], P(None, None, ('rep', 'blk'), None, 'tp')
The draws below stay inside these ranges and needn't reach their ends.
Inputs may be any that keep to these rules, and one draw needn't show every extreme that they name: `page_owner`: requests are numbered replica by replica, 4 to a replica. Each request has exactly one page with page_tail 1, which is used and lies among the pages of its own replica; other pages of a request may lie on any replica. `page_used`: every page with page_tail 1 is used. `page_fill`: A used page with page_tail 0 is full; a page with page_tail 1 holds fewer than 32 tokens; an unused page holds 0.
All inputs are finite; a program needn't handle non-finite values.
Results may differ from the reference program's by a relative error of at most 0.012.
The reference program's roundings to bfloat16 on the way (of `normed`, `mlp_act`, `queries` and `attended`) count: a program that leaves them out, or rounds other values in their place, can miss the bound.
Values may be sent and summed in bfloat16 or wider, within the bound.
A program may use at most 64 MiB of HBM per device.

```python
import jax
import jax.numpy as jnp
from jax import lax

D = 2048
H = 32
HD = 64
ROT = 32
FF = 8192
LAYERS = 2
PAGE = 32
SLOTS = 8
REQ_REP = 4
REQS = 16
SLOTS_REP = 16
SLOTS_ALL = 64


def page_layout(key):
    base = jax.random.fold_in(key, 11)
    keys = jax.random.split(base, 9)
    rep_total = SLOTS_ALL // SLOTS_REP
    slot_ids = jnp.arange(SLOTS_ALL, dtype=jnp.int32)
    slot_rep = slot_ids // SLOTS_REP
    rank_keys = jax.random.split(keys[0], rep_total)
    ranks = jax.vmap(lambda k: jnp.argsort(jax.random.permutation(k, SLOTS_REP), stable=True))(rank_keys)
    ranks = ranks.reshape(-1).astype(jnp.int32)
    tail = (ranks < REQ_REP).astype(jnp.int32)
    popular = jax.random.permutation(keys[1], REQ_REP).astype(jnp.int32)
    draw_a = jax.random.randint(keys[2], (SLOTS_ALL,), 0, REQ_REP)
    draw_b = jax.random.randint(keys[3], (SLOTS_ALL,), 0, REQ_REP)
    draw_c = jax.random.randint(keys[4], (SLOTS_ALL,), 0, REQ_REP)
    pick = popular[jnp.minimum(jnp.minimum(draw_a, draw_b), draw_c)]
    step_away = jax.random.randint(keys[6], (SLOTS_ALL,), 0, max(rep_total - 1, 1))
    owner_rep = (slot_rep + 1 + step_away) % rep_total
    owner = jnp.where(tail == 1, slot_rep * REQ_REP + ranks, owner_rep * REQ_REP + pick).astype(jnp.int32)
    used_rand = (jax.random.randint(keys[7], (SLOTS_ALL,), 0, 4) != 0).astype(jnp.int32)
    used_rand = jnp.where(ranks == REQ_REP, 0, used_rand)
    used = jnp.where(tail == 1, 1, used_rand).astype(jnp.int32)
    tail_fill = jax.random.randint(keys[8], (SLOTS_ALL,), 0, PAGE)
    fill = jnp.where(tail == 1, tail_fill, jnp.where(used == 1, PAGE, 0)).astype(jnp.int32)
    return (owner, used, fill, tail)


def draw_page_owner(key, part):
    return page_layout(key)[0]


def draw_page_used(key, part):
    return page_layout(key)[1]


def draw_page_fill(key, part):
    return page_layout(key)[2]


def draw_page_tail(key, part):
    return page_layout(key)[3]


def draw_hidden(key, part):
    keys = jax.random.split(jax.random.fold_in(key, 23), 2)
    column = jnp.arange(D, dtype=jnp.float32) / D
    rough = jax.random.uniform(keys[1], (D,), jnp.float32, 0.6, 1.6)
    scale_col = 0.5 * jnp.exp(jnp.log(3.0) * column) * rough
    values = jax.random.normal(keys[0], (REQS, D), jnp.float32) * scale_col[None, :]
    return jnp.clip(values, -64.0, 64.0).astype(jnp.bfloat16)


def draw_caches(key, part):
    keys = jax.random.split(jax.random.fold_in(key, 31), 1)
    shape = (LAYERS, 2, SLOTS_ALL, PAGE, H * HD)
    values = jnp.clip(jax.random.normal(keys[0], shape, jnp.float32), -6.0, 6.0)
    return values.astype(jnp.bfloat16)


def plant(entries, stream_key, least, top_value):
    index_at = [jax.random.randint(jax.random.fold_in(stream_key, axis), (), 0, length) for axis, length in enumerate(entries.shape)]
    main_axis = entries.shape.index(max(entries.shape))
    neighbour = index_at[:main_axis] + [(index_at[main_axis] + 1) % entries.shape[main_axis]] + index_at[main_axis + 1:]
    return entries.at[tuple(index_at)].set(least).at[tuple(neighbour)].set(top_value)


def shard_levels(own_key, shape, shards, smallest, high):
    def one(position, shards_of):
        heights = jax.random.uniform(jax.random.fold_in(jax.random.fold_in(own_key, 6), position), (shards_of,), jnp.float32, smallest / len(shards), high / len(shards))
        return jnp.repeat(jnp.exp(heights), shape[position] // shards_of).reshape((-1,) + (1,) * (len(shape) - position - 1))

    loudness = one(*shards[0])
    for cut in shards[1:]:
        loudness = loudness * one(*cut)
    return loudness


def normal_values(stream_key, extent, spread, most, shards=(), held_as=jnp.bfloat16):
    entries = jax.random.normal(stream_key, extent, jnp.float32) * spread
    if len(shards) > 0:
        entries = shard_levels(stream_key, extent, shards, -0.22, 0.18) * entries
    return jnp.clip(entries, min=-most, max=most).astype(held_as)


def setup_inputs(seed: int = 0) -> dict:
    splits = jax.random.split(jax.random.key(seed), 13)
    return {
        "hidden": draw_hidden(jax.random.fold_in(splits[12], 71), 0),
        "ln_gain": jnp.clip(1.0 + 0.18 * jax.random.normal(splits[1], (LAYERS, D), jnp.float32), 0.1, 1.9),
        "w_qkv": normal_values(splits[2], (LAYERS, D, 3, H * HD), D ** -0.5, 0.125, ((1, 2), (3, 4))),
        "w_fc1": normal_values(splits[3], (LAYERS, D, FF), D ** -0.5, 0.125, ((1, 2), (2, 4))),
        "w_out": normal_values(splits[4], (LAYERS, H * HD, D), (H * HD) ** -0.5, 0.125, ((1, 4), (2, 2))),
        "w_fc2": normal_values(splits[5], (LAYERS, FF, D), FF ** -0.5, 0.0625, ((1, 4), (2, 2))),
        "caches": draw_caches(jax.random.fold_in(splits[12], 71), 0),
        "page_owner": draw_page_owner(jax.random.fold_in(splits[12], 71), 0),
        "page_used": draw_page_used(jax.random.fold_in(splits[12], 71), 0),
        "page_fill": draw_page_fill(jax.random.fold_in(splits[12], 71), 0),
        "page_tail": draw_page_tail(jax.random.fold_in(splits[12], 71), 0),
        "positions": plant(jax.random.randint(splits[11], (REQS,), 0, 4096), jax.random.fold_in(splits[11], 1), 0, 4095).astype(jnp.int32),
    }


EPSILON = 1e-05
LOWEST = -1e+30

def rotate_heads(tensor, positions):
    half_rot = ROT // 2
    steps_f = jnp.arange(half_rot, dtype=jnp.float32)
    inverse = 10000.0 ** (-2.0 * steps_f / ROT)
    angles = positions.astype(jnp.float32)[:, None] * inverse[None, :]
    cosine = jnp.cos(angles)[:, None, :]
    sine_val = jnp.sin(angles)[:, None, :]
    first_half = tensor[..., :half_rot]
    second_half = tensor[..., half_rot:ROT]
    return jnp.concatenate([first_half * cosine - second_half * sine_val, second_half * cosine + first_half * sine_val, tensor[..., ROT:]], axis=-1)

def page_partials(items):
    query_rows, key_pages, value_pages, valid = items
    scores = jnp.einsum('shd,sphd->shp', query_rows.astype(jnp.float32), key_pages.astype(jnp.float32)) * HD ** (-0.5)
    scores = jnp.where(valid[:, None, :], scores, LOWEST)
    highest = lax.optimization_barrier(jnp.max(scores, axis=-1))
    weights = jnp.where(valid[:, None, :], jnp.exp(scores - highest[..., None]), 0.0)
    totals = lax.optimization_barrier(jnp.sum(weights, axis=-1))
    rounded = weights.astype(jnp.bfloat16)
    outputs = jnp.einsum('shp,sphd->shd', rounded.astype(jnp.float32), value_pages.astype(jnp.float32))
    return (highest, totals, outputs)

def reference(hidden, ln_gain, w_qkv, w_fc1, w_out, w_fc2, caches, page_owner, page_used, page_fill, page_tail, positions):
    width = H * HD
    offsets = jnp.arange(PAGE, dtype=jnp.int32)
    is_tail = page_tail == 1
    is_used = page_used == 1
    write_at = (offsets[None, :] == page_fill[:, None]) & is_tail[:, None]
    valid = is_used[:, None] & (offsets[None, :] < (page_fill + page_tail)[:, None])
    state = hidden
    cache_list = []
    for layer in range(LAYERS):
        resid = state.astype(jnp.float32)
        average = lax.optimization_barrier(jnp.mean(resid, axis=-1, keepdims=True))
        centered = resid - average
        variance = lax.optimization_barrier(jnp.mean(centered * centered, axis=-1, keepdims=True))
        normed = (centered * lax.rsqrt(variance + EPSILON) * ln_gain[layer][None, :]).astype(jnp.bfloat16)
        qkv = jnp.dot(normed, w_qkv[layer].reshape(D, 3 * width), preferred_element_type=jnp.float32).reshape(REQS, 3, H, HD)
        inner = jnp.dot(normed, w_fc1[layer], preferred_element_type=jnp.float32)
        mlp_act = jax.nn.gelu(inner, approximate=True).astype(jnp.bfloat16)
        queries = rotate_heads(qkv[:, 0], positions).astype(jnp.bfloat16).reshape(REQS, width)
        new_keys = rotate_heads(qkv[:, 1], positions).astype(jnp.bfloat16).reshape(REQS, width)
        new_values = qkv[:, 2].astype(jnp.bfloat16).reshape(REQS, width)
        key_pages = jnp.where(write_at[:, :, None], new_keys[page_owner][:, None, :], caches[layer, 0])
        value_pages = jnp.where(write_at[:, :, None], new_values[page_owner][:, None, :], caches[layer, 1])
        cache_list.append(jnp.stack([key_pages, value_pages]))
        query_rows = queries[page_owner]
        highest, totals, outputs = lax.map(page_partials, (query_rows.reshape(-1, SLOTS, H, HD), key_pages.reshape(-1, SLOTS, PAGE, H, HD), value_pages.reshape(-1, SLOTS, PAGE, H, HD), valid.reshape(-1, SLOTS, PAGE)))
        highest = highest.reshape(SLOTS_ALL, H)
        totals = totals.reshape(SLOTS_ALL, H)
        outputs = outputs.reshape(SLOTS_ALL, H, HD)
        masked_high = jnp.where(is_used[:, None], highest, LOWEST)
        request_high = jax.ops.segment_max(masked_high, page_owner, num_segments=REQS)
        scale_w = jnp.where(is_used[:, None], jnp.exp(highest - request_high[page_owner]), 0.0)
        denom = jax.ops.segment_sum(totals * scale_w, page_owner, num_segments=REQS)
        numer = jax.ops.segment_sum(outputs * scale_w[..., None], page_owner, num_segments=REQS)
        attended = (numer / denom[..., None]).reshape(REQS, width).astype(jnp.bfloat16)
        attn_part = jnp.dot(attended, w_out[layer], preferred_element_type=jnp.float32)
        mlp_part = jnp.dot(mlp_act, w_fc2[layer], preferred_element_type=jnp.float32)
        state = (resid + attn_part + mlp_part).astype(jnp.bfloat16)
    return (state, jnp.stack(cache_list))
```

```python
import functools

import jax
import jax.numpy as jnp
import numpy as np
from jax import lax
from jax.experimental import pallas as pl
from jax.experimental.pallas import tpu as pltpu
from jax.sharding import PartitionSpec as P

HD = 64
ROT = 32
LAYERS = 2
PAGE = 32
EPSILON = 1e-05
LOWEST = -1e30
MESH = pl.DeviceIdType.MESH
UNROLL = 8


def each(start, stop, body):
    if stop - start <= UNROLL:
        for k in range(start, stop):
            body(k)
    else:
        lax.fori_loop(start, stop, lambda k, c: (body(k), c)[1], 0)


def fold_sum(start, stop, body, carry):
    if stop - start <= UNROLL:
        for k in range(start, stop):
            carry = body(k, carry)
        return carry
    return lax.fori_loop(start, stop, body, carry)


def lane_iota(shape):
    return lax.broadcasted_iota(jnp.int32, shape, len(shape) - 1)


def row_iota(shape):
    return lax.broadcasted_iota(jnp.int32, shape, len(shape) - 2)


def kernel(
    n_rep, n_blk, n_tp,
    owner_ref, used_ref, fill_ref, tail_ref, pos_ref,
    hidden_ref, gain_ref, freq_ref,
    wqkv_hbm, wfc1_hbm, wout_hbm, wfc2_hbm, cache_hbm,
    state_ref, fresh_ref,
    wqkv, wfc1, wout, wfc2, cache,
    buf_a, buf_i, buf_q, msg, buf_b, buf_c, mlp_acc, act_ref,
    w_sem, a_send, a_recv, i_send, i_recv, q_send, q_recv, b_send, b_recv, c_send, c_recv,
):
    f32, bf16 = jnp.float32, jnp.bfloat16
    rows, model = hidden_ref.shape
    full_model = model * n_blk
    slots = owner_ref.shape[0]
    width = wout.shape[1]
    heads = width // HD
    n_ff = wfc1.shape[1]
    reqs = rows * n_rep
    n_all = n_rep * n_blk
    half = width // 2
    my_rep, my_blk, my_tp = lax.axis_index("rep"), lax.axis_index("blk"), lax.axis_index("tp")
    my_flat = my_rep * n_blk + my_blk
    ff_half = n_ff // 2

    local = []

    def bring(src, dst):
        copy = pltpu.make_async_copy(src, dst, w_sem.at[len(local)])
        copy.start()
        local.append(copy)
        return copy

    got = []
    for l in range(LAYERS):
        g = {}
        g["qkv"] = [bring(wqkv_hbm.at[l, j], wqkv.at[l, j]) for j in range(3)]
        g["fc1"] = [
            bring(wfc1_hbm.at[l, :, pl.ds(c * width, width)], wfc1.at[l, c]) for c in range(n_ff)
        ]
        g["cache"] = [bring(cache_hbm.at[l, i], cache.at[l, i]) for i in range(2)]
        g["fc2"] = [
            bring(wfc2_hbm.at[l, pl.ds(i * ff_half * width, ff_half * width), :], wfc2.at[l, i])
            for i in range(2)
        ]
        g["out"] = [bring(wout_hbm.at[l], wout.at[l])]
        got.append(g)

    def flat_peer(k):
        to = lax.rem(my_flat + k, n_all)
        return {"rep": to // n_blk, "blk": lax.rem(to, n_blk)}

    def blk_peer(k):
        return {"blk": lax.rem(my_blk + k, n_blk)}

    def rep_peer(k):
        return {"rep": lax.rem(my_rep + k, n_rep)}

    def tp_peer(k):
        return {"tp": lax.rem(my_tp + k, n_tp)}

    barrier = pltpu.get_barrier_semaphore()
    each(1, n_all, lambda k: pl.semaphore_signal(
        barrier, inc=1, device_id=flat_peer(k), device_id_type=MESH))
    each(1, n_tp, lambda k: pl.semaphore_signal(
        barrier, inc=1, device_id=tp_peer(k), device_id_type=MESH))

    def remote(src, dst, ssem, rsem, peer):
        return pltpu.make_async_remote_copy(
            src_ref=src, dst_ref=dst, send_sem=ssem, recv_sem=rsem,
            device_id=peer, device_id_type=MESH)

    def copy_a(l):
        return lambda k: remote(
            buf_a.at[l, 0], buf_a.at[l, k], a_send.at[l, k], a_recv.at[l, k], blk_peer(k))

    def copy_i(l):
        return lambda k: remote(
            buf_i.at[l, 0], buf_i.at[l, k], i_send.at[l, k], i_recv.at[l, k], blk_peer(k))

    def copy_q(l):
        return lambda k: remote(
            buf_q.at[l, 0], buf_q.at[l, k], q_send.at[l, k], q_recv.at[l, k], rep_peer(k))

    def copy_b(l):
        return lambda k: remote(
            msg.at[l, lax.rem(my_flat + k, n_all) // n_blk], buf_b.at[l, k],
            b_send.at[l, k], b_recv.at[l, k], flat_peer(k))

    def copy_c(l):
        return lambda k: remote(
            buf_c.at[l, 0], buf_c.at[l, k], c_send.at[l, k], c_recv.at[l, k], tp_peer(k))

    feature = lax.rem(lane_iota((2 * rows, width)), HD)
    small = (2 * rows, 128)
    posv = jnp.zeros(small, f32)
    for r in range(rows):
        posv = jnp.where(
            lax.rem(row_iota(small), rows) == r, pos_ref[r].astype(f32), posv)
    angles = posv * freq_ref[...]
    cosine = jnp.concatenate([jnp.cos(angles)] * (width // 128), axis=1)
    sine = jnp.concatenate([jnp.sin(angles)] * (width // 128), axis=1)
    sine = jnp.where(feature < ROT // 2, -sine, sine)

    columns = slots * PAGE
    lanes = lane_iota((1, columns))
    col_owner = jnp.full((1, columns), -1, jnp.int32)
    home = jnp.full((slots, width), -1, jnp.int32)
    write_pos = []
    for s in range(slots):
        limit = jnp.where(used_ref[s] == 1, fill_ref[s] + tail_ref[s], 0)
        here = (lanes >= s * PAGE) & (lanes < s * PAGE + limit)
        col_owner = jnp.where(here, owner_ref[s], col_owner)
        home_row = jnp.where(tail_ref[s] == 1, owner_ref[s] - my_rep * rows, -1)
        home = jnp.where(row_iota((slots, width)) == s, home_row, home)
        write_pos.append(jnp.where(tail_ref[s] == 1, fill_ref[s], -1))

    head_of_lane = lane_iota((1, width)) // HD

    def expand(stat):
        out = jnp.broadcast_to(stat[:, 0:1], (stat.shape[0], width))
        for h in range(1, heads):
            out = jnp.where(head_of_lane == h, stat[:, h:h + 1], out)
        return out

    def fold(x):
        return jnp.concatenate([x[:, :x.shape[1] // 2], x[:, x.shape[1] // 2:]], axis=0)

    def unfold(x):
        return jnp.concatenate([x[:rows], x[rows:]], axis=1)

    state = hidden_ref[...].astype(f32)
    for l in range(LAYERS):
        g = got[l]
        own_mean = jnp.sum(state, axis=1, keepdims=True) / model
        centered = state - own_mean
        own_square = jnp.sum(centered * centered, axis=1, keepdims=True)
        gain = gain_ref[l:l + 1, :]
        gain_hi = gain.astype(bf16).astype(f32)
        gain_lo = gain - gain_hi
        lhs = jnp.concatenate(
            [centered * gain, gain_hi, gain_lo, jnp.zeros((2 * rows - rows - 2, model), f32)],
            axis=0).astype(bf16)
        stat_lane = lane_iota((rows, width))
        stats = jnp.where(stat_lane < 128, own_mean, own_square)
        buf_a[l, 0, 3] = jnp.concatenate([stats, jnp.zeros((rows, width), f32)], axis=0)
        for j in range(3):
            g["qkv"][j].wait()
            buf_a[l, 0, j] = jnp.dot(lhs, wqkv[l, j], preferred_element_type=f32)
        if l == 0:
            pl.semaphore_wait(barrier, n_all - 1 + n_tp - 1)
        each(1, n_blk, lambda k: copy_a(l)(k).start())
        for c in range(n_ff):
            g["fc1"][c].wait()
            buf_i[l, 0, c] = jnp.dot(lhs, wfc1[l, c], preferred_element_type=f32)
        each(1, n_blk, lambda k: copy_i(l)(k).start())

        each(1, n_blk, lambda k: copy_a(l)(k).wait_recv())
        mean = fold_sum(0, n_blk, lambda k, t: t + buf_a[l, k, 3, 0:rows, 0:1],
                        jnp.zeros((rows, 1), f32)) / n_blk

        def add_square(k, total):
            off = buf_a[l, k, 3, 0:rows, 0:1] - mean
            return total + (buf_a[l, k, 3, 0:rows, 128:129] + model * (off * off))

        square = fold_sum(0, n_blk, add_square, jnp.zeros((rows, 1), f32))
        scale = lax.rsqrt(square / full_model + EPSILON)

        def finish(buf, j):
            def add(k, total):
                off = buf_a[l, k, 3, 0:rows, 0:1] - mean
                block = buf[l, k, j]
                gained = block[rows:rows + 1] + block[rows + 1:rows + 2]
                return total + (block[0:rows] + off * gained)

            return fold_sum(0, n_blk, add, jnp.zeros((rows, width), f32)) * scale

        qk = jnp.concatenate([finish(buf_a, 0), finish(buf_a, 1)], axis=0)
        turned = jnp.where(
            feature < ROT // 2,
            pltpu.roll(qk, width - ROT // 2, 1),
            pltpu.roll(qk, ROT // 2, 1))
        qk = (qk * cosine + turned * sine).astype(bf16).astype(f32)
        buf_q[l, 0] = fold(qk[:rows])
        each(1, n_rep, lambda k: copy_q(l)(k).start())
        new_k = qk[rows:]
        new_v = finish(buf_a, 2).astype(bf16).astype(f32)

        for i, new in ((0, new_k), (1, new_v)):
            fresh = jnp.zeros((slots, width), f32)
            for r in range(rows):
                fresh = jnp.where(home == r, new[r:r + 1], fresh)
            fresh_ref[l, i] = fresh
            g["cache"][i].wait()
            for s in range(slots):
                page = cache[l, i, s].astype(f32)
                page = jnp.where(
                    row_iota((PAGE, width)) == write_pos[s], fresh[s:s + 1], page)
                cache[l, i, s] = page.astype(bf16)

        each(1, n_blk, lambda k: copy_i(l)(k).wait_recv())
        for c in range(n_ff):
            act = jax.nn.gelu(finish(buf_i, c), approximate=True)
            act_ref[c] = jnp.concatenate([act, jnp.zeros((rows, width), f32)], axis=0).astype(bf16)
        g["fc2"][0].wait()
        mlp_acc[...] = jnp.dot(
            jnp.concatenate([act_ref[c] for c in range(ff_half)], axis=1),
            wfc2[l, 0], preferred_element_type=f32)

        each(1, n_rep, lambda k: copy_q(l)(k).wait_recv())
        queries = jnp.concatenate(
            [unfold(buf_q[l, lax.rem(my_rep - t + n_rep, n_rep)]) for t in range(n_rep)], axis=0)
        by_head = jnp.concatenate(
            [jnp.where(head_of_lane == h, queries, 0.0) for h in range(heads)], axis=0
        ).astype(bf16)
        keys = cache[l, 0].reshape(columns, width)
        values = cache[l, 1].reshape(columns, width)
        scores = lax.dot_general(
            by_head, keys, (((1,), (1,)), ((), ())), preferred_element_type=f32) * HD ** (-0.5)
        mask = lax.rem(row_iota((heads * reqs, columns)), reqs) == col_owner
        scores = jnp.where(mask, scores, LOWEST)
        highest = jnp.max(scores, axis=1, keepdims=True)
        weights = jnp.where(mask, jnp.exp(scores - highest), 0.0)
        totals = jnp.sum(weights, axis=1, keepdims=True)
        spread = jnp.dot(weights.astype(bf16), values, preferred_element_type=f32)
        out = spread[0:reqs]
        stat_shape = (reqs, 128)
        high_stat = jnp.zeros(stat_shape, f32)
        total_stat = jnp.ones(stat_shape, f32)
        for h in range(heads):
            part = slice(h * reqs, (h + 1) * reqs)
            if h > 0:
                out = jnp.where(head_of_lane == h, spread[part], out)
            high_stat = jnp.where(lane_iota(stat_shape) == h, highest[part], high_stat)
            total_stat = jnp.where(lane_iota(stat_shape) == h, totals[part], total_stat)
        for r in range(n_rep):
            part = slice(r * rows, (r + 1) * rows)
            msg[l, r, :, 0:half] = fold(out[part])
            msg[l, r, :, half:half + 128] = jnp.concatenate(
                [high_stat[part], total_stat[part]], axis=0)
        each(1, n_all, lambda k: copy_b(l)(k).start())
        buf_b[l, 0] = msg[l, my_rep]

        g["fc2"][1].wait()
        mlp_acc[...] += jnp.dot(
            jnp.concatenate([act_ref[c] for c in range(ff_half, n_ff)], axis=1),
            wfc2[l, 1], preferred_element_type=f32)

        each(1, n_all, lambda k: copy_b(l)(k).wait_recv())
        top = fold_sum(
            0, n_all,
            lambda k, t: jnp.maximum(t, buf_b[l, k, 0:rows, half:half + 128]),
            jnp.full((rows, 128), LOWEST, f32))

        def merge(k, carry):
            denom, numer = carry
            factor = jnp.exp(buf_b[l, k, 0:rows, half:half + 128] - top)
            denom = denom + factor * buf_b[l, k, rows:2 * rows, half:half + 128]
            numer = numer + expand(factor) * unfold(buf_b[l, k, :, 0:half])
            return denom, numer

        denom, numer = fold_sum(
            0, n_all, merge, (jnp.zeros((rows, 128), f32), jnp.zeros((rows, width), f32)))
        attended = numer / expand(denom)
        attended = jnp.concatenate(
            [attended, jnp.zeros((rows, width), f32)], axis=0).astype(bf16)
        g["out"][0].wait()
        branch = (
            jnp.dot(attended, wout[l], preferred_element_type=f32) + mlp_acc[...])[0:rows]
        folded = model >= 256
        if folded:
            buf_c[l, 0] = fold(branch)
        else:
            buf_c[l, 0] = jnp.zeros(buf_c.shape[2:], f32)
            buf_c[l, 0, 0:rows, 0:model] = branch
        each(1, n_tp, lambda k: copy_c(l)(k).start())
        each(1, n_tp, lambda k: copy_c(l)(k).wait_recv())
        total = buf_c[l, lax.rem(my_tp + n_tp, n_tp)]
        for t in range(1, n_tp):
            total = total + buf_c[l, lax.rem(my_tp - t + n_tp, n_tp)]
        total = unfold(total) if folded else total[0:rows, 0:model]
        state = (state + total).astype(bf16).astype(f32)

    state_ref[...] = state
    for l in range(LAYERS):
        each(1, n_blk, lambda k: copy_a(l)(k).wait_send())
        each(1, n_blk, lambda k: copy_i(l)(k).wait_send())
        each(1, n_rep, lambda k: copy_q(l)(k).wait_send())
        each(1, n_all, lambda k: copy_b(l)(k).wait_send())
        each(1, n_tp, lambda k: copy_c(l)(k).wait_send())


def frequencies(rows):
    feature = np.arange(128) % HD
    power = 10000.0 ** (-2.0 * (feature % (ROT // 2)) / ROT)
    return np.tile(np.where(feature < ROT, power, 0.0).astype(np.float32)[None, :], (rows, 1))


def per_device(
    hidden, ln_gain, w_qkv, w_fc1, w_out, w_fc2, caches,
    page_owner, page_used, page_fill, page_tail, positions,
):
    n_rep, n_blk, n_tp = (lax.axis_size(a) for a in ("rep", "blk", "tp"))
    f32, bf16 = jnp.float32, jnp.bfloat16
    rows, model = hidden.shape
    slots = page_owner.shape[0]
    width = w_out.shape[1]
    n_ff = w_fc1.shape[2] // width
    n_all = n_rep * n_blk
    wq = jnp.transpose(w_qkv, (0, 2, 1, 3))
    c_width = model // 2 if model >= 256 else 128
    smem = pl.BlockSpec(memory_space=pltpu.SMEM)
    vmem = pl.BlockSpec(memory_space=pltpu.VMEM)
    anywhere = pl.BlockSpec(memory_space=pl.ANY)
    dma = pltpu.SemaphoreType.DMA
    n_copies = LAYERS * (3 + n_ff + 2 + 2 + 1)
    state, fresh = pl.pallas_call(
        functools.partial(kernel, n_rep, n_blk, n_tp),
        out_shape=(
            jax.ShapeDtypeStruct((rows, model), f32),
            jax.ShapeDtypeStruct((LAYERS, 2, slots, width), f32),
        ),
        in_specs=[smem] * 5 + [vmem] * 3 + [anywhere] * 5,
        out_specs=(vmem, vmem),
        scratch_shapes=[
            pltpu.VMEM((LAYERS, 3, model, width), bf16),
            pltpu.VMEM((LAYERS, n_ff, model, width), bf16),
            pltpu.VMEM((LAYERS, width, model), bf16),
            pltpu.VMEM((LAYERS, 2, n_ff // 2 * width, model), bf16),
            pltpu.VMEM((LAYERS, 2, slots, PAGE, width), bf16),
            pltpu.VMEM((LAYERS, n_blk, 4, 2 * rows, width), f32),
            pltpu.VMEM((LAYERS, n_blk, n_ff, 2 * rows, width), f32),
            pltpu.VMEM((LAYERS, n_rep, 2 * rows, width // 2), f32),
            pltpu.VMEM((LAYERS, n_rep, 2 * rows, width // 2 + 128), f32),
            pltpu.VMEM((LAYERS, n_all, 2 * rows, width // 2 + 128), f32),
            pltpu.VMEM((LAYERS, n_tp, 2 * rows, c_width), f32),
            pltpu.VMEM((2 * rows, model), f32),
            pltpu.VMEM((n_ff, 2 * rows, width), bf16),
            dma((n_copies,)),
            dma((LAYERS, n_blk)), dma((LAYERS, n_blk)),
            dma((LAYERS, n_blk)), dma((LAYERS, n_blk)),
            dma((LAYERS, n_rep)), dma((LAYERS, n_rep)),
            dma((LAYERS, n_all)), dma((LAYERS, n_all)),
            dma((LAYERS, n_tp)), dma((LAYERS, n_tp)),
        ],
        compiler_params=pltpu.CompilerParams(
            collective_id=0, has_side_effects=True, vmem_limit_bytes=56 * 2**20),
        name="decode_layers",
    )(
        page_owner, page_used, page_fill, page_tail, positions,
        hidden, ln_gain, jnp.asarray(frequencies(2 * rows)),
        wq, w_fc1, w_out, w_fc2, caches,
    )
    offsets = jnp.arange(PAGE, dtype=jnp.int32)
    write_at = (offsets[None, :] == page_fill[:, None]) & (page_tail == 1)[:, None]
    caches_out = jnp.where(
        write_at[None, None, :, :, None], fresh[:, :, :, None, :].astype(bf16), caches)
    return (state.astype(bf16), caches_out)


def solution(mesh):
    in_specs = (
        P("rep", "blk"),
        P(None, "blk"),
        P(None, "blk", None, "tp"),
        P(None, "blk", "tp"),
        P(None, "tp", "blk"),
        P(None, "tp", "blk"),
        P(None, None, ("rep", "blk"), None, "tp"),
        P(("rep", "blk")),
        P(("rep", "blk")),
        P(("rep", "blk")),
        P(("rep", "blk")),
        P("rep"),
    )
    out_specs = (P("rep", "blk"), P(None, None, ("rep", "blk"), None, "tp"))
    return jax.shard_map(
        per_device, mesh=mesh, in_specs=in_specs, out_specs=out_specs, check_vma=False
    )
```

```python
import functools

import jax
import jax.numpy as jnp
import numpy as np
from jax import lax
from jax.experimental import pallas as pl
from jax.experimental.pallas import tpu as pltpu
from jax.sharding import PartitionSpec as P

HD = 64
ROT = 32
LAYERS = 2
PAGE = 32
EPSILON = 1e-05
LOWEST = -1e30
MESH = pl.DeviceIdType.MESH
UNROLL = 8


def each(start, stop, body):
    if stop - start <= UNROLL:
        for k in range(start, stop):
            body(k)
    else:
        lax.fori_loop(start, stop, lambda k, c: (body(k), c)[1], 0)


def fold_sum(start, stop, body, carry):
    if stop - start <= UNROLL:
        for k in range(start, stop):
            carry = body(k, carry)
        return carry
    return lax.fori_loop(start, stop, body, carry)


def lane_iota(shape):
    return lax.broadcasted_iota(jnp.int32, shape, len(shape) - 1)


def row_iota(shape):
    return lax.broadcasted_iota(jnp.int32, shape, len(shape) - 2)


def kernel(
    n_rep, n_blk, n_tp,
    owner_ref, used_ref, fill_ref, tail_ref, pos_ref,
    hidden_ref, gain_ref, freq_ref,
    wqkv_hbm, wfc1_hbm, wout_hbm, wfc2_hbm, cache_hbm,
    state_ref, pages_ref,
    wqkv, wfc1, wout, wfc2, cache,
    buf_a, buf_i, buf_q, msg, buf_b, buf_c, mlp_acc, act_ref, mask_ref,
    w_sem, o_sem, a_send, a_recv, i_send, i_recv, q_send, q_recv, b_send, b_recv, c_send, c_recv,
):
    f32, bf16 = jnp.float32, jnp.bfloat16
    rows, model = hidden_ref.shape
    full_model = model * n_blk
    slots = owner_ref.shape[0]
    width = wout.shape[1]
    heads = width // HD
    n_ff = wfc1.shape[2] // width
    reqs = rows * n_rep
    n_all = n_rep * n_blk
    half = width // 2
    my_rep, my_blk, my_tp = lax.axis_index("rep"), lax.axis_index("blk"), lax.axis_index("tp")
    my_flat = my_rep * n_blk + my_blk
    ff_half = n_ff // 2

    def flat_peer(k):
        to = lax.rem(my_flat + k, n_all)
        return {"rep": to // n_blk, "blk": lax.rem(to, n_blk)}

    def blk_peer(k):
        return {"blk": lax.rem(my_blk + k, n_blk)}

    def rep_peer(k):
        return {"rep": lax.rem(my_rep + k, n_rep)}

    def tp_peer(k):
        return {"tp": lax.rem(my_tp + k, n_tp)}

    barrier = pltpu.get_barrier_semaphore()
    each(1, n_all, lambda k: pl.semaphore_signal(
        barrier, inc=1, device_id=flat_peer(k), device_id_type=MESH))
    each(1, n_tp, lambda k: pl.semaphore_signal(
        barrier, inc=1, device_id=tp_peer(k), device_id_type=MESH))

    local = []

    def bring(src, dst):
        copy = pltpu.make_async_copy(src, dst, w_sem.at[len(local)])
        copy.start()
        local.append(copy)
        return copy

    def bring_layer(l, pieces):
        g = {}
        g["qkv"] = [bring(wqkv_hbm.at[l, j], wqkv.at[l, j]) for j in range(3)]
        step = n_ff // pieces
        g["fc1"] = [
            bring(wfc1_hbm.at[l, :, pl.ds(c * width, step * width)],
                  wfc1.at[l, :, pl.ds(c * width, step * width)])
            if c % step == 0 else None for c in range(n_ff)
        ]
        g["cache"] = [
            bring(cache_hbm.at[l, i], cache.at[l, i, pl.ds(0, slots)]) for i in range(2)]
        g["fc2"] = [
            bring(wfc2_hbm.at[l, pl.ds(i * ff_half * width, ff_half * width), :], wfc2.at[l, i])
            for i in range(2)
        ]
        g["out"] = [bring(wout_hbm.at[l], wout.at[l])]
        return g

    got = {0: bring_layer(0, n_ff // 2)}

    def remote(src, dst, ssem, rsem, peer):
        return pltpu.make_async_remote_copy(
            src_ref=src, dst_ref=dst, send_sem=ssem, recv_sem=rsem,
            device_id=peer, device_id_type=MESH)

    def copy_a(l):
        return lambda k: remote(
            buf_a.at[l, 0], buf_a.at[l, k], a_send.at[l, k], a_recv.at[l, k], blk_peer(k))

    def copy_i(l):
        return lambda k: remote(
            buf_i.at[l, 0], buf_i.at[l, k], i_send.at[l, k], i_recv.at[l, k], blk_peer(k))

    def copy_q(l):
        return lambda k: remote(
            buf_q.at[l, 0], buf_q.at[l, k], q_send.at[l, k], q_recv.at[l, k], rep_peer(k))

    def copy_b(l):
        return lambda k: remote(
            msg.at[l, lax.rem(my_flat + k, n_all) // n_blk], buf_b.at[l, k],
            b_send.at[l, k], b_recv.at[l, k], flat_peer(k))

    def copy_c(l):
        return lambda k: remote(
            buf_c.at[l, 0], buf_c.at[l, k], c_send.at[l, k], c_recv.at[l, k], tp_peer(k))

    feature = lax.rem(lane_iota((2 * rows, width)), HD)
    small = (2 * rows, 128)
    posv = jnp.zeros(small, f32)
    for r in range(rows):
        posv = jnp.where(
            lax.rem(row_iota(small), rows) == r, pos_ref[r].astype(f32), posv)
    angles = posv * freq_ref[...]
    cosine = jnp.concatenate([jnp.cos(angles)] * (width // 128), axis=1)
    sine = jnp.concatenate([jnp.sin(angles)] * (width // 128), axis=1)
    sine = jnp.where(feature < ROT // 2, -sine, sine)

    extra = cache.shape[2] - slots
    columns = (slots + extra) * PAGE
    lanes = lane_iota((1, columns))
    col_owner = jnp.full((1, columns), -1, jnp.int32)
    home = jnp.full((slots, width), -1, jnp.int32)
    write_pos = []
    for s in range(slots):
        limit = jnp.where(used_ref[s] == 1, fill_ref[s], 0)
        here = (lanes >= s * PAGE) & (lanes < s * PAGE + limit)
        col_owner = jnp.where(here, owner_ref[s], col_owner)
        home_row = jnp.where(tail_ref[s] == 1, owner_ref[s] - my_rep * rows, -1)
        home = jnp.where(row_iota((slots, width)) == s, home_row, home)
        new_lane = jnp.where(tail_ref[s] == 1, slots * PAGE + home_row, -1)
        col_owner = jnp.where(lanes == new_lane, owner_ref[s], col_owner)
        write_pos.append(jnp.where(tail_ref[s] == 1, fill_ref[s], -1))
    mask_ref[...] = jnp.where(
        lax.rem(row_iota((heads * reqs, columns)), reqs) == col_owner, 1.0, 0.0)
    for l in range(LAYERS):
        for i in range(2):
            for s in range(slots, slots + extra):
                cache[l, i, s] = jnp.zeros((PAGE, width), bf16)

    head_of_lane = lane_iota((1, width)) // HD

    def expand(stat):
        out = jnp.broadcast_to(stat[:, 0:1], (stat.shape[0], width))
        for h in range(1, heads):
            out = jnp.where(head_of_lane == h, stat[:, h:h + 1], out)
        return out

    def fold(x):
        return jnp.concatenate([x[:, :x.shape[1] // 2], x[:, x.shape[1] // 2:]], axis=0)

    def unfold(x):
        return jnp.concatenate([x[:rows], x[rows:]], axis=1)

    wide = model >= 512

    def fold_c(x):
        if wide:
            return jnp.concatenate(
                [x[:, c * (model // 4):(c + 1) * (model // 4)] for c in range(4)], axis=0)
        x = jnp.concatenate([x, jnp.zeros((16 - rows, model), f32)], axis=0)
        if model < buf_c.shape[3]:
            x = jnp.concatenate([x, jnp.zeros((16, buf_c.shape[3] - model), f32)], axis=1)
        return x

    def unfold_c(x):
        if wide:
            return jnp.concatenate(
                [x[c * rows:(c + 1) * rows] for c in range(4)], axis=1)
        return x[0:rows, 0:model]

    out_copies = []
    state = hidden_ref[...].astype(f32)
    for l in range(LAYERS):
        g = got[l]
        own_mean = jnp.sum(state, axis=1, keepdims=True) / model
        centered = state - own_mean
        own_square = jnp.sum(centered * centered, axis=1, keepdims=True)
        gain = gain_ref[l:l + 1, :]
        gain_hi = gain.astype(bf16).astype(f32)
        gain_lo = gain - gain_hi
        lhs = jnp.concatenate(
            [centered * gain, gain_hi, gain_lo, jnp.zeros((2 * rows - rows - 2, model), f32)],
            axis=0).astype(bf16)
        stat_lane = lane_iota((rows, width))
        stats = jnp.where(stat_lane < 128, own_mean, own_square)
        buf_a[l, 0, 3] = jnp.concatenate([stats, jnp.zeros((rows, width), f32)], axis=0)
        for j in range(3):
            g["qkv"][j].wait()
            buf_a[l, 0, j] = jnp.dot(lhs, wqkv[l, j], preferred_element_type=f32)
        if l == 0:
            pl.semaphore_wait(barrier, n_all - 1 + n_tp - 1)
        each(1, n_blk, lambda k: copy_a(l)(k).start())
        for c in range(n_ff):
            if g["fc1"][c] is not None:
                g["fc1"][c].wait()
            buf_i[l, 0, c] = jnp.dot(
                lhs, wfc1[l, :, c * width:(c + 1) * width], preferred_element_type=f32)
        each(1, n_blk, lambda k: copy_i(l)(k).start())
        if l + 1 < LAYERS:
            got[l + 1] = bring_layer(l + 1, 1)

        each(1, n_blk, lambda k: copy_a(l)(k).wait_recv())
        mean = fold_sum(0, n_blk, lambda k, t: t + buf_a[l, k, 3, 0:rows, 0:1],
                        jnp.zeros((rows, 1), f32)) / n_blk

        def add_square(k, total):
            off = buf_a[l, k, 3, 0:rows, 0:1] - mean
            return total + (buf_a[l, k, 3, 0:rows, 128:129] + model * (off * off))

        square = fold_sum(0, n_blk, add_square, jnp.zeros((rows, 1), f32))
        scale = lax.rsqrt(square / full_model + EPSILON)

        def finish(buf, j):
            def add(k, total):
                off = buf_a[l, k, 3, 0:rows, 0:1] - mean
                block = buf[l, k, j]
                gained = block[rows:rows + 1] + block[rows + 1:rows + 2]
                return total + (block[0:rows] + off * gained)

            return fold_sum(0, n_blk, add, jnp.zeros((rows, width), f32)) * scale

        qk = jnp.concatenate([finish(buf_a, 0), finish(buf_a, 1)], axis=0)
        turned = jnp.where(
            feature < ROT // 2,
            pltpu.roll(qk, width - ROT // 2, 1),
            pltpu.roll(qk, ROT // 2, 1))
        qk = (qk * cosine + turned * sine).astype(bf16).astype(f32)
        buf_q[l, 0] = fold(qk[:rows])
        each(1, n_rep, lambda k: copy_q(l)(k).start())
        new_k = qk[rows:]
        new_v = finish(buf_a, 2).astype(bf16).astype(f32)

        new = (new_k, new_v)
        for i in range(2):
            cache[l, i, slots, 0:16] = jnp.concatenate(
                [new[i], jnp.zeros((16 - rows, width), f32)], axis=0).astype(bf16)

        each(1, n_blk, lambda k: copy_i(l)(k).wait_recv())
        for c in range(n_ff):
            act = jax.nn.gelu(finish(buf_i, c), approximate=True)
            act_ref[c] = jnp.concatenate([act, jnp.zeros((rows, width), f32)], axis=0).astype(bf16)
        g["fc2"][0].wait()
        mlp_acc[...] = jnp.dot(
            jnp.concatenate([act_ref[c] for c in range(ff_half)], axis=1),
            wfc2[l, 0], preferred_element_type=f32)

        each(1, n_rep, lambda k: copy_q(l)(k).wait_recv())
        queries = jnp.concatenate(
            [unfold(buf_q[l, lax.rem(my_rep - t + n_rep, n_rep)]) for t in range(n_rep)], axis=0)
        by_head = jnp.concatenate(
            [jnp.where(head_of_lane == h, queries, 0.0) for h in range(heads)], axis=0
        ).astype(bf16)
        for i in range(2):
            g["cache"][i].wait()
        keys = cache[l, 0].reshape(columns, width)
        values = cache[l, 1].reshape(columns, width)
        scores = lax.dot_general(
            by_head, keys, (((1,), (1,)), ((), ())), preferred_element_type=f32) * HD ** (-0.5)
        mask = mask_ref[...] > 0.0
        scores = jnp.where(mask, scores, LOWEST)
        highest = jnp.max(scores, axis=1, keepdims=True)
        weights = jnp.where(mask, jnp.exp(scores - highest), 0.0)
        totals = jnp.sum(weights, axis=1, keepdims=True)
        spread = jnp.dot(weights.astype(bf16), values, preferred_element_type=f32)
        out = spread[0:reqs]
        stat_shape = (reqs, 128)
        high_stat = jnp.zeros(stat_shape, f32)
        total_stat = jnp.ones(stat_shape, f32)
        for h in range(heads):
            part = slice(h * reqs, (h + 1) * reqs)
            if h > 0:
                out = jnp.where(head_of_lane == h, spread[part], out)
            high_stat = jnp.where(lane_iota(stat_shape) == h, highest[part], high_stat)
            total_stat = jnp.where(lane_iota(stat_shape) == h, totals[part], total_stat)
        for r in range(n_rep):
            part = slice(r * rows, (r + 1) * rows)
            msg[l, r, :, 0:half] = fold(out[part])
            msg[l, r, :, half:half + 128] = jnp.concatenate(
                [high_stat[part], total_stat[part]], axis=0)
        each(1, n_all, lambda k: copy_b(l)(k).start())
        buf_b[l, 0] = msg[l, my_rep]

        g["fc2"][1].wait()
        mlp_acc[...] += jnp.dot(
            jnp.concatenate([act_ref[c] for c in range(ff_half, n_ff)], axis=1),
            wfc2[l, 1], preferred_element_type=f32)

        each(1, n_all, lambda k: copy_b(l)(k).wait_recv())
        top = fold_sum(
            0, n_all,
            lambda k, t: jnp.maximum(t, buf_b[l, k, 0:rows, half:half + 128]),
            jnp.full((rows, 128), LOWEST, f32))

        def merge(k, carry):
            denom, numer = carry
            factor = jnp.exp(buf_b[l, k, 0:rows, half:half + 128] - top)
            denom = denom + factor * buf_b[l, k, rows:2 * rows, half:half + 128]
            numer = numer + expand(factor) * unfold(buf_b[l, k, :, 0:half])
            return denom, numer

        denom, numer = fold_sum(
            0, n_all, merge, (jnp.zeros((rows, 128), f32), jnp.zeros((rows, width), f32)))
        attended = numer / expand(denom)
        attended = jnp.concatenate(
            [attended, jnp.zeros((rows, width), f32)], axis=0).astype(bf16)
        g["out"][0].wait()
        branch = (
            jnp.dot(attended, wout[l], preferred_element_type=f32) + mlp_acc[...])[0:rows]
        buf_c[l, 0] = fold_c(branch).astype(bf16)
        each(1, n_tp, lambda k: copy_c(l)(k).start())

        for i in range(2):
            fresh = jnp.zeros((slots, width), f32)
            for r in range(rows):
                fresh = jnp.where(home == r, new[i][r:r + 1], fresh)
            for s in range(slots):
                page = cache[l, i, s].astype(f32)
                page = jnp.where(
                    row_iota((PAGE, width)) == write_pos[s], fresh[s:s + 1], page)
                cache[l, i, s] = page.astype(bf16)
            out_copies.append(pltpu.make_async_copy(
                cache.at[l, i, pl.ds(0, slots)], pages_ref.at[l, i], o_sem.at[l, i]))
            out_copies[-1].start()

        each(1, n_tp, lambda k: copy_c(l)(k).wait_recv())
        total = buf_c[l, lax.rem(my_tp + n_tp, n_tp)].astype(f32)
        for t in range(1, n_tp):
            total = total + buf_c[l, lax.rem(my_tp - t + n_tp, n_tp)].astype(f32)
        total = unfold_c(total)
        state = (state + total).astype(bf16).astype(f32)

    state_ref[...] = state.astype(bf16)
    for copy in out_copies:
        copy.wait()
    for l in range(LAYERS):
        each(1, n_blk, lambda k: copy_a(l)(k).wait_send())
        each(1, n_blk, lambda k: copy_i(l)(k).wait_send())
        each(1, n_rep, lambda k: copy_q(l)(k).wait_send())
        each(1, n_all, lambda k: copy_b(l)(k).wait_send())
        each(1, n_tp, lambda k: copy_c(l)(k).wait_send())


def frequencies(rows):
    feature = np.arange(128) % HD
    power = 10000.0 ** (-2.0 * (feature % (ROT // 2)) / ROT)
    return np.tile(np.where(feature < ROT, power, 0.0).astype(np.float32)[None, :], (rows, 1))


def per_device(
    hidden, ln_gain, w_qkv, w_fc1, w_out, w_fc2, caches,
    page_owner, page_used, page_fill, page_tail, positions,
):
    n_rep, n_blk, n_tp = (lax.axis_size(a) for a in ("rep", "blk", "tp"))
    f32, bf16 = jnp.float32, jnp.bfloat16
    rows, model = hidden.shape
    slots = page_owner.shape[0]
    width = w_out.shape[1]
    n_ff = w_fc1.shape[2] // width
    n_all = n_rep * n_blk
    wq = jnp.transpose(w_qkv, (0, 2, 1, 3))
    c_width = model // 4 if model >= 512 else max(model, 128)
    extra = 128 // PAGE
    smem = pl.BlockSpec(memory_space=pltpu.SMEM)
    vmem = pl.BlockSpec(memory_space=pltpu.VMEM)
    anywhere = pl.BlockSpec(memory_space=pl.ANY)
    dma = pltpu.SemaphoreType.DMA
    n_copies = LAYERS * (3 + n_ff + 2 + 2 + 1)
    return pl.pallas_call(
        functools.partial(kernel, n_rep, n_blk, n_tp),
        out_shape=(
            jax.ShapeDtypeStruct((rows, model), bf16),
            jax.ShapeDtypeStruct(caches.shape, bf16),
        ),
        in_specs=[smem] * 5 + [vmem] * 3 + [anywhere] * 5,
        out_specs=(vmem, anywhere),
        scratch_shapes=[
            pltpu.VMEM((LAYERS, 3, model, width), bf16),
            pltpu.VMEM((LAYERS, model, n_ff * width), bf16),
            pltpu.VMEM((LAYERS, width, model), bf16),
            pltpu.VMEM((LAYERS, 2, n_ff // 2 * width, model), bf16),
            pltpu.VMEM((LAYERS, 2, slots + extra, PAGE, width), bf16),
            pltpu.VMEM((LAYERS, n_blk, 4, 2 * rows, width), f32),
            pltpu.VMEM((LAYERS, n_blk, n_ff, 2 * rows, width), f32),
            pltpu.VMEM((LAYERS, n_rep, 2 * rows, width // 2), f32),
            pltpu.VMEM((LAYERS, n_rep, 2 * rows, width // 2 + 128), f32),
            pltpu.VMEM((LAYERS, n_all, 2 * rows, width // 2 + 128), f32),
            pltpu.VMEM((LAYERS, n_tp, 16, c_width), bf16),
            pltpu.VMEM((2 * rows, model), f32),
            pltpu.VMEM((n_ff, 2 * rows, width), bf16),
            pltpu.VMEM((width // HD * rows * n_rep, (slots + extra) * PAGE), f32),
            dma((n_copies,)), dma((LAYERS, 2)),
            dma((LAYERS, n_blk)), dma((LAYERS, n_blk)),
            dma((LAYERS, n_blk)), dma((LAYERS, n_blk)),
            dma((LAYERS, n_rep)), dma((LAYERS, n_rep)),
            dma((LAYERS, n_all)), dma((LAYERS, n_all)),
            dma((LAYERS, n_tp)), dma((LAYERS, n_tp)),
        ],
        compiler_params=pltpu.CompilerParams(
            collective_id=0, has_side_effects=True, vmem_limit_bytes=56 * 2**20),
        name="decode_layers",
    )(
        page_owner, page_used, page_fill, page_tail, positions,
        hidden, ln_gain, jnp.asarray(frequencies(2 * rows)),
        wq, w_fc1, w_out, w_fc2, caches,
    )


def solution(mesh):
    in_specs = (
        P("rep", "blk"),
        P(None, "blk"),
        P(None, "blk", None, "tp"),
        P(None, "blk", "tp"),
        P(None, "tp", "blk"),
        P(None, "tp", "blk"),
        P(None, None, ("rep", "blk"), None, "tp"),
        P(("rep", "blk")),
        P(("rep", "blk")),
        P(("rep", "blk")),
        P(("rep", "blk")),
        P("rep"),
    )
    out_specs = (P("rep", "blk"), P(None, None, ("rep", "blk"), None, "tp"))
    return jax.shard_map(
        per_device, mesh=mesh, in_specs=in_specs, out_specs=out_specs, check_vma=False
    )
```

```python
import functools

import jax
import jax.numpy as jnp
import numpy as np
from jax import lax
from jax.experimental import pallas as pl
from jax.experimental.pallas import tpu as pltpu
from jax.sharding import PartitionSpec as P

HD = 64
ROT = 32
LAYERS = 2
PAGE = 32
EPSILON = 1e-05
LOWEST = -1e30
MESH = pl.DeviceIdType.MESH
UNROLL = 8


def each(start, stop, body):
    if stop - start <= UNROLL:
        for k in range(start, stop):
            body(k)
    else:
        lax.fori_loop(start, stop, lambda k, c: (body(k), c)[1], 0)


def fold_sum(start, stop, body, carry):
    if stop - start <= UNROLL:
        for k in range(start, stop):
            carry = body(k, carry)
        return carry
    return lax.fori_loop(start, stop, body, carry)


def lane_iota(shape):
    return lax.broadcasted_iota(jnp.int32, shape, len(shape) - 1)


def row_iota(shape):
    return lax.broadcasted_iota(jnp.int32, shape, len(shape) - 2)


def kernel(
    n_rep, n_blk, n_tp,
    owner_ref, used_ref, fill_ref, tail_ref, pos_ref,
    hidden_ref, gain_ref, freq_ref,
    wqkv_hbm, wfc1_hbm, wout_hbm, wfc2_hbm, cache_hbm,
    state_ref, fresh_ref, bound_hbm,
    wqkv, wfc1, wout, wfc2, cache,
    buf_a, buf_i, buf_q, msg, buf_b, buf_c, mlp_acc, act_ref, mask_ref, bound_ref,
    w_sem, o_sem, a_send, a_recv, i_send, i_recv, q_send, q_recv, b_send, b_recv, c_send, c_recv,
):
    f32, bf16 = jnp.float32, jnp.bfloat16
    rows, model = hidden_ref.shape
    full_model = model * n_blk
    slots = owner_ref.shape[0]
    width = wout.shape[1]
    heads = width // HD
    n_ff = wfc1.shape[2] // width
    reqs = rows * n_rep
    n_all = n_rep * n_blk
    quarter = width // 4
    my_rep, my_blk, my_tp = lax.axis_index("rep"), lax.axis_index("blk"), lax.axis_index("tp")
    my_flat = my_rep * n_blk + my_blk
    ff_half = n_ff // 2

    def flat_peer(k):
        to = lax.rem(my_flat + k, n_all)
        return {"rep": to // n_blk, "blk": lax.rem(to, n_blk)}

    def blk_peer(k):
        return {"blk": lax.rem(my_blk + k, n_blk)}

    def rep_peer(k):
        return {"rep": lax.rem(my_rep + k, n_rep)}

    def tp_peer(k):
        return {"tp": lax.rem(my_tp + k, n_tp)}

    barrier = pltpu.get_barrier_semaphore()
    each(1, n_all, lambda k: pl.semaphore_signal(
        barrier, inc=1, device_id=flat_peer(k), device_id_type=MESH))
    each(1, n_tp, lambda k: pl.semaphore_signal(
        barrier, inc=1, device_id=tp_peer(k), device_id_type=MESH))

    local = []

    def bring(src, dst):
        copy = pltpu.make_async_copy(src, dst, w_sem.at[len(local)])
        copy.start()
        local.append(copy)
        return copy

    def bring_layer(l, pieces):
        g = {}
        g["qkv"] = [bring(wqkv_hbm.at[l, j], wqkv.at[l, j]) for j in range(3)]
        step = n_ff // pieces
        g["fc1"] = [
            bring(wfc1_hbm.at[l, :, pl.ds(c * width, step * width)],
                  wfc1.at[l, :, pl.ds(c * width, step * width)])
            if c % step == 0 else None for c in range(n_ff)
        ]
        g["cache"] = [
            bring(cache_hbm.at[l, i], cache.at[l, i, pl.ds(0, slots)]) for i in range(2)]
        g["fc2"] = [
            bring(wfc2_hbm.at[l, pl.ds(i * ff_half * width, ff_half * width), :], wfc2.at[l, i])
            for i in range(2)
        ]
        g["out"] = [bring(wout_hbm.at[l], wout.at[l])]
        return g

    got = {0: bring_layer(0, n_ff // 2)}

    def remote(src, dst, ssem, rsem, peer):
        return pltpu.make_async_remote_copy(
            src_ref=src, dst_ref=dst, send_sem=ssem, recv_sem=rsem,
            device_id=peer, device_id_type=MESH)

    def copy_a(l, part):
        piece = pl.ds(2 * part, 2)
        return lambda k: remote(
            buf_a.at[l, 0, piece], buf_a.at[l, k, piece],
            a_send.at[l, k, part], a_recv.at[l, k, part], blk_peer(k))

    def copy_i(l):
        return lambda k: remote(
            buf_i.at[l, 0], buf_i.at[l, k], i_send.at[l, k], i_recv.at[l, k], blk_peer(k))

    def copy_q(l):
        return lambda k: remote(
            buf_q.at[l, 0], buf_q.at[l, k], q_send.at[l, k], q_recv.at[l, k], rep_peer(k))

    def copy_b(l):
        return lambda k: remote(
            msg.at[l, lax.rem(my_flat + k, n_all) // n_blk], buf_b.at[l, k],
            b_send.at[l, k], b_recv.at[l, k], flat_peer(k))

    def copy_c(l):
        return lambda k: remote(
            buf_c.at[l, 0], buf_c.at[l, k], c_send.at[l, k], c_recv.at[l, k], tp_peer(k))

    feature = lax.rem(lane_iota((2 * rows, width)), HD)
    small = (2 * rows, 128)
    posv = jnp.zeros(small, f32)
    for r in range(rows):
        posv = jnp.where(
            lax.rem(row_iota(small), rows) == r, pos_ref[r].astype(f32), posv)
    angles = posv * freq_ref[...]
    cosine = jnp.concatenate([jnp.cos(angles)] * (width // 128), axis=1)
    sine = jnp.concatenate([jnp.sin(angles)] * (width // 128), axis=1)
    sine = jnp.where(feature < ROT // 2, -sine, sine)

    extra = cache.shape[2] - slots
    columns = (slots + extra) * PAGE
    lanes = lane_iota((1, columns))
    col_owner = jnp.full((1, columns), -1, jnp.int32)
    home = jnp.full((slots, width), -1, jnp.int32)
    for s in range(slots):
        limit = jnp.where(used_ref[s] == 1, fill_ref[s], 0)
        here = (lanes >= s * PAGE) & (lanes < s * PAGE + limit)
        col_owner = jnp.where(here, owner_ref[s], col_owner)
        home_row = jnp.where(tail_ref[s] == 1, owner_ref[s] - my_rep * rows, -1)
        home = jnp.where(row_iota((slots, width)) == s, home_row, home)
        new_lane = jnp.where(tail_ref[s] == 1, slots * PAGE + home_row, -1)
        col_owner = jnp.where(lanes == new_lane, owner_ref[s], col_owner)
        write_pos = jnp.where(tail_ref[s] == 1, fill_ref[s], -1)
        bound_ref[s] = jnp.where(
            row_iota((PAGE, width)) == write_pos, -jnp.inf, jnp.inf).astype(bf16)
    bound_copy = pltpu.make_async_copy(bound_ref, bound_hbm, o_sem.at[0])
    bound_copy.start()
    mask_ref[...] = jnp.where(
        lax.rem(row_iota((heads * reqs, columns)), reqs) == col_owner, 1.0, 0.0)
    for l in range(LAYERS):
        for i in range(2):
            for s in range(slots, slots + extra):
                cache[l, i, s] = jnp.zeros((PAGE, width), bf16)

    head_of_lane = lane_iota((1, width)) // HD

    def expand(stat):
        out = jnp.broadcast_to(stat[:, 0:1], (stat.shape[0], width))
        for h in range(1, heads):
            out = jnp.where(head_of_lane == h, stat[:, h:h + 1], out)
        return out

    def fold(x):
        part = x.shape[1] // 4
        return jnp.concatenate([x[:, c * part:(c + 1) * part] for c in range(4)], axis=0)

    def unfold(x):
        x = x.astype(f32)
        return jnp.concatenate([x[c * rows:(c + 1) * rows] for c in range(4)], axis=1)

    def split(x):
        high = x.astype(bf16).astype(f32)
        return high, (x - high).astype(bf16).astype(f32)

    wide = model >= 512

    def fold_c(x):
        if wide:
            return fold(x)
        x = jnp.concatenate([x, jnp.zeros((16 - rows, model), f32)], axis=0)
        if model < buf_c.shape[3]:
            x = jnp.concatenate([x, jnp.zeros((16, buf_c.shape[3] - model), f32)], axis=1)
        return x

    def unfold_c(x):
        if wide:
            return unfold(x)
        return x[0:rows, 0:model]

    state = hidden_ref[...].astype(f32)
    for l in range(LAYERS):
        g = got[l]
        own_mean = jnp.sum(state, axis=1, keepdims=True) / model
        centered = state - own_mean
        own_square = jnp.sum(centered * centered, axis=1, keepdims=True)
        gain = gain_ref[l:l + 1, :]
        gain_hi = gain.astype(bf16).astype(f32)
        gain_lo = gain - gain_hi
        lhs = jnp.concatenate(
            [centered * gain, gain_hi, gain_lo, jnp.zeros((2 * rows - rows - 2, model), f32)],
            axis=0).astype(bf16)
        stat_lane = lane_iota((rows, width))
        stats = jnp.where(stat_lane < 128, own_mean, own_square)
        buf_a[l, 0, 0] = jnp.concatenate([stats, jnp.zeros((rows, width), f32)], axis=0)

        def project(j):
            g["qkv"][j].wait()
            buf_a[l, 0, 1 + j] = jnp.dot(lhs, wqkv[l, j], preferred_element_type=f32)

        def project_ff(c):
            if g["fc1"][c] is not None:
                g["fc1"][c].wait()
            buf_i[l, 0, c] = jnp.dot(
                lhs, wfc1[l, :, c * width:(c + 1) * width], preferred_element_type=f32)

        project(0)
        if l == 0:
            pl.semaphore_wait(barrier, n_all - 1 + n_tp - 1)
        each(1, n_blk, lambda k: copy_a(l, 0)(k).start())
        project(1)
        project(2)
        each(1, n_blk, lambda k: copy_a(l, 1)(k).start())
        for c in range(ff_half):
            project_ff(c)

        each(1, n_blk, lambda k: copy_a(l, 0)(k).wait_recv())
        mean = fold_sum(0, n_blk, lambda k, t: t + buf_a[l, k, 0, 0:rows, 0:1],
                        jnp.zeros((rows, 1), f32)) / n_blk

        def add_square(k, total):
            off = buf_a[l, k, 0, 0:rows, 0:1] - mean
            return total + (buf_a[l, k, 0, 0:rows, 128:129] + model * (off * off))

        square = fold_sum(0, n_blk, add_square, jnp.zeros((rows, 1), f32))
        scale = lax.rsqrt(square / full_model + EPSILON)

        def finish(buf, j):
            def add(k, total):
                off = buf_a[l, k, 0, 0:rows, 0:1] - mean
                block = buf[l, k, j]
                gained = block[rows:rows + 1] + block[rows + 1:rows + 2]
                return total + (block[0:rows] + off * gained)

            return fold_sum(0, n_blk, add, jnp.zeros((rows, width), f32)) * scale

        def rotate(x):
            turned = jnp.where(
                feature < ROT // 2,
                pltpu.roll(x, width - ROT // 2, 1),
                pltpu.roll(x, ROT // 2, 1))
            return (x * cosine + turned * sine).astype(bf16).astype(f32)

        blank = jnp.zeros((rows, width), f32)
        own_queries = rotate(jnp.concatenate([finish(buf_a, 1), blank], axis=0))[:rows]
        buf_q[l, 0] = fold(own_queries).astype(bf16)
        each(1, n_rep, lambda k: copy_q(l)(k).start())
        for c in range(ff_half, n_ff):
            project_ff(c)
        each(1, n_blk, lambda k: copy_i(l)(k).start())
        if l + 1 < LAYERS:
            got[l + 1] = bring_layer(l + 1, 1)
        each(1, n_blk, lambda k: copy_a(l, 1)(k).wait_recv())
        new_k = rotate(jnp.concatenate([finish(buf_a, 2), blank], axis=0))[:rows]
        new_v = finish(buf_a, 3).astype(bf16).astype(f32)
        new = (new_k, new_v)
        for i in range(2):
            cache[l, i, slots, 0:16] = jnp.concatenate(
                [new[i], jnp.zeros((16 - rows, width), f32)], axis=0).astype(bf16)

        each(1, n_blk, lambda k: copy_i(l)(k).wait_recv())
        for c in range(n_ff):
            act = jax.nn.gelu(finish(buf_i, c), approximate=True)
            act_ref[c] = jnp.concatenate([act, jnp.zeros((rows, width), f32)], axis=0).astype(bf16)
        g["fc2"][0].wait()
        mlp_acc[...] = jnp.dot(
            jnp.concatenate([act_ref[c] for c in range(ff_half)], axis=1),
            wfc2[l, 0], preferred_element_type=f32)

        each(1, n_rep, lambda k: copy_q(l)(k).wait_recv())
        queries = jnp.concatenate(
            [unfold(buf_q[l, lax.rem(my_rep - t + n_rep, n_rep)]) for t in range(n_rep)], axis=0)
        by_head = jnp.concatenate(
            [jnp.where(head_of_lane == h, queries, 0.0) for h in range(heads)], axis=0
        ).astype(bf16)
        for i in range(2):
            g["cache"][i].wait()
        keys = cache[l, 0].reshape(columns, width)
        values = cache[l, 1].reshape(columns, width)
        scores = lax.dot_general(
            by_head, keys, (((1,), (1,)), ((), ())), preferred_element_type=f32) * HD ** (-0.5)
        mask = mask_ref[...] > 0.0
        scores = jnp.where(mask, scores, LOWEST)
        high_pieces = split(jnp.max(scores, axis=1, keepdims=True))
        highest = high_pieces[0] + high_pieces[1]
        weights = jnp.where(mask, jnp.exp(scores - highest), 0.0)
        totals = jnp.sum(weights, axis=1, keepdims=True)
        spread = jnp.dot(weights.astype(bf16), values, preferred_element_type=f32)
        out = spread[0:reqs]
        stat_shape = (reqs, 128)
        stats = [jnp.zeros(stat_shape, f32), jnp.zeros(stat_shape, f32),
                 jnp.ones(stat_shape, f32), jnp.zeros(stat_shape, f32)]
        for h in range(heads):
            part = slice(h * reqs, (h + 1) * reqs)
            if h > 0:
                out = jnp.where(head_of_lane == h, spread[part], out)
            for i, piece in enumerate(high_pieces + split(totals)):
                stats[i] = jnp.where(lane_iota(stat_shape) == h, piece[part], stats[i])
        for r in range(n_rep):
            part = slice(r * rows, (r + 1) * rows)
            msg[l, r] = jnp.concatenate(
                [fold(out[part]), jnp.concatenate([stat[part] for stat in stats], axis=0)],
                axis=1).astype(bf16)
        each(1, n_all, lambda k: copy_b(l)(k).start())
        buf_b[l, 0] = msg[l, my_rep]

        g["fc2"][1].wait()
        mlp_acc[...] += jnp.dot(
            jnp.concatenate([act_ref[c] for c in range(ff_half, n_ff)], axis=1),
            wfc2[l, 1], preferred_element_type=f32)

        each(1, n_all, lambda k: copy_b(l)(k).wait_recv())

        def stat_of(k, first):
            stat = buf_b[l, k, :, quarter:quarter + 128].astype(f32)
            return stat[first * rows:(first + 1) * rows] + stat[(first + 1) * rows:(first + 2) * rows]

        top = fold_sum(
            0, n_all, lambda k, t: jnp.maximum(t, stat_of(k, 0)),
            jnp.full((rows, 128), LOWEST, f32))

        def merge(k, carry):
            denom, numer = carry
            factor = jnp.exp(stat_of(k, 0) - top)
            denom = denom + factor * stat_of(k, 2)
            numer = numer + expand(factor) * unfold(buf_b[l, k, :, 0:quarter])
            return denom, numer

        denom, numer = fold_sum(
            0, n_all, merge, (jnp.zeros((rows, 128), f32), jnp.zeros((rows, width), f32)))
        attended = numer / expand(denom)
        attended = jnp.concatenate(
            [attended, jnp.zeros((rows, width), f32)], axis=0).astype(bf16)
        g["out"][0].wait()
        branch = (
            jnp.dot(attended, wout[l], preferred_element_type=f32) + mlp_acc[...])[0:rows]
        buf_c[l, 0] = fold_c(branch).astype(bf16)
        each(1, n_tp, lambda k: copy_c(l)(k).start())

        for i in range(2):
            fresh = jnp.zeros((slots, width), f32)
            for r in range(rows):
                fresh = jnp.where(home == r, new[i][r:r + 1], fresh)
            fresh_ref[l, i] = fresh.astype(bf16)

        each(1, n_tp, lambda k: copy_c(l)(k).wait_recv())
        total = buf_c[l, lax.rem(my_tp + n_tp, n_tp)].astype(f32)
        for t in range(1, n_tp):
            total = total + buf_c[l, lax.rem(my_tp - t + n_tp, n_tp)].astype(f32)
        total = unfold_c(total)
        state = (state + total).astype(bf16).astype(f32)

    state_ref[...] = state
    bound_copy.wait()
    for l in range(LAYERS):
        each(1, n_blk, lambda k: copy_a(l, 0)(k).wait_send())
        each(1, n_blk, lambda k: copy_a(l, 1)(k).wait_send())
        each(1, n_blk, lambda k: copy_i(l)(k).wait_send())
        each(1, n_rep, lambda k: copy_q(l)(k).wait_send())
        each(1, n_all, lambda k: copy_b(l)(k).wait_send())
        each(1, n_tp, lambda k: copy_c(l)(k).wait_send())


def frequencies(rows):
    feature = np.arange(128) % HD
    power = 10000.0 ** (-2.0 * (feature % (ROT // 2)) / ROT)
    return np.tile(np.where(feature < ROT, power, 0.0).astype(np.float32)[None, :], (rows, 1))


def per_device(
    hidden, ln_gain, w_qkv, w_fc1, w_out, w_fc2, caches,
    page_owner, page_used, page_fill, page_tail, positions,
):
    n_rep, n_blk, n_tp = (lax.axis_size(a) for a in ("rep", "blk", "tp"))
    f32, bf16 = jnp.float32, jnp.bfloat16
    rows, model = hidden.shape
    slots = page_owner.shape[0]
    width = w_out.shape[1]
    n_ff = w_fc1.shape[2] // width
    n_all = n_rep * n_blk
    wq = jnp.transpose(w_qkv, (0, 2, 1, 3))
    c_width = model // 4 if model >= 512 else max(model, 128)
    extra = 128 // PAGE
    smem = pl.BlockSpec(memory_space=pltpu.SMEM)
    vmem = pl.BlockSpec(memory_space=pltpu.VMEM)
    anywhere = pl.BlockSpec(memory_space=pl.ANY)
    dma = pltpu.SemaphoreType.DMA
    n_copies = LAYERS * (3 + n_ff + 2 + 2 + 1)
    state, fresh, bound = pl.pallas_call(
        functools.partial(kernel, n_rep, n_blk, n_tp),
        out_shape=(
            jax.ShapeDtypeStruct((rows, model), f32),
            jax.ShapeDtypeStruct((LAYERS, 2, slots, width), bf16),
            jax.ShapeDtypeStruct((slots, PAGE, width), bf16),
        ),
        in_specs=[smem] * 5 + [vmem] * 3 + [anywhere] * 5,
        out_specs=(vmem, vmem, anywhere),
        scratch_shapes=[
            pltpu.VMEM((LAYERS, 3, model, width), bf16),
            pltpu.VMEM((LAYERS, model, n_ff * width), bf16),
            pltpu.VMEM((LAYERS, width, model), bf16),
            pltpu.VMEM((LAYERS, 2, n_ff // 2 * width, model), bf16),
            pltpu.VMEM((LAYERS, 2, slots + extra, PAGE, width), bf16),
            pltpu.VMEM((LAYERS, n_blk, 4, 2 * rows, width), f32),
            pltpu.VMEM((LAYERS, n_blk, n_ff, 2 * rows, width), f32),
            pltpu.VMEM((LAYERS, n_rep, 4 * rows, width // 4), bf16),
            pltpu.VMEM((LAYERS, n_rep, 4 * rows, width // 4 + 128), bf16),
            pltpu.VMEM((LAYERS, n_all, 4 * rows, width // 4 + 128), bf16),
            pltpu.VMEM((LAYERS, n_tp, 16, c_width), bf16),
            pltpu.VMEM((2 * rows, model), f32),
            pltpu.VMEM((n_ff, 2 * rows, width), bf16),
            pltpu.VMEM((width // HD * rows * n_rep, (slots + extra) * PAGE), f32),
            pltpu.VMEM((slots, PAGE, width), bf16),
            dma((n_copies,)), dma((1,)),
            dma((LAYERS, n_blk, 2)), dma((LAYERS, n_blk, 2)),
            dma((LAYERS, n_blk)), dma((LAYERS, n_blk)),
            dma((LAYERS, n_rep)), dma((LAYERS, n_rep)),
            dma((LAYERS, n_all)), dma((LAYERS, n_all)),
            dma((LAYERS, n_tp)), dma((LAYERS, n_tp)),
        ],
        compiler_params=pltpu.CompilerParams(
            collective_id=0, has_side_effects=True, vmem_limit_bytes=56 * 2**20),
        name="decode_layers",
    )(
        page_owner, page_used, page_fill, page_tail, positions,
        hidden, ln_gain, jnp.asarray(frequencies(2 * rows)),
        wq, w_fc1, w_out, w_fc2, caches,
    )
    caches_out = jnp.where(caches < bound[None, None], caches, fresh[:, :, :, None, :])
    return (state.astype(bf16), caches_out)


def solution(mesh):
    in_specs = (
        P("rep", "blk"),
        P(None, "blk"),
        P(None, "blk", None, "tp"),
        P(None, "blk", "tp"),
        P(None, "tp", "blk"),
        P(None, "tp", "blk"),
        P(None, None, ("rep", "blk"), None, "tp"),
        P(("rep", "blk")),
        P(("rep", "blk")),
        P(("rep", "blk")),
        P(("rep", "blk")),
        P("rep"),
    )
    out_specs = (P("rep", "blk"), P(None, None, ("rep", "blk"), None, "tp"))
    return jax.shard_map(
        per_device, mesh=mesh, in_specs=in_specs, out_specs=out_specs, check_vma=False
    )
```

```python
import functools

import jax
import jax.numpy as jnp
import numpy as np
from jax import lax
from jax.experimental import pallas as pl
from jax.experimental.pallas import tpu as pltpu
from jax.sharding import PartitionSpec as P

HD = 64
ROT = 32
LAYERS = 2
PAGE = 32
EPSILON = 1e-05
LOWEST = -1e30
MESH = pl.DeviceIdType.MESH
UNROLL = 8


def each(start, stop, body):
    if stop - start <= UNROLL:
        for k in range(start, stop):
            body(k)
    else:
        lax.fori_loop(start, stop, lambda k, c: (body(k), c)[1], 0)


def fold_sum(start, stop, body, carry):
    if stop - start <= UNROLL:
        for k in range(start, stop):
            carry = body(k, carry)
        return carry
    return lax.fori_loop(start, stop, body, carry)


def lane_iota(shape):
    return lax.broadcasted_iota(jnp.int32, shape, len(shape) - 1)


def row_iota(shape):
    return lax.broadcasted_iota(jnp.int32, shape, len(shape) - 2)


def kernel(
    n_rep, n_blk, n_tp,
    owner_ref, used_ref, fill_ref, tail_ref, pos_ref,
    hidden_ref, gain_ref, freq_ref,
    wqkv_hbm, wfc1_hbm, wout_hbm, wfc2_hbm, cache_hbm,
    state_ref, fresh_ref, bound_hbm,
    wqkv, wfc1, wout, wfc2, cache,
    buf_a, buf_i, buf_q, msg, buf_b, buf_c, buf_x, msg_m, buf_m, mask_ref, bound_ref,
    w_sem, o_sem, a_send, a_recv, i_send, i_recv, q_send, q_recv, b_send, b_recv, c_send, c_recv,
    x_send, x_recv, m_send, m_recv,
):
    f32, bf16 = jnp.float32, jnp.bfloat16
    rows, model = hidden_ref.shape
    full_model = model * n_blk
    slots = owner_ref.shape[0]
    width = wout.shape[1]
    heads = width // HD
    ff = wfc1.shape[2]
    reqs = rows * n_rep
    n_all = n_rep * n_blk
    quarter = width // 4
    my_rep, my_blk, my_tp = lax.axis_index("rep"), lax.axis_index("blk"), lax.axis_index("tp")
    my_flat = my_rep * n_blk + my_blk
    ff_at = pl.multiple_of(my_rep * ff, ff)

    def flat_peer(k):
        to = lax.rem(my_flat + k, n_all)
        return {"rep": to // n_blk, "blk": lax.rem(to, n_blk)}

    def blk_peer(k):
        return {"blk": lax.rem(my_blk + k, n_blk)}

    def rep_peer(k):
        return {"rep": lax.rem(my_rep + k, n_rep)}

    def tp_peer(k):
        return {"tp": lax.rem(my_tp + k, n_tp)}

    barrier = pltpu.get_barrier_semaphore()
    each(1, n_all, lambda k: pl.semaphore_signal(
        barrier, inc=1, device_id=flat_peer(k), device_id_type=MESH))
    each(1, n_tp, lambda k: pl.semaphore_signal(
        barrier, inc=1, device_id=tp_peer(k), device_id_type=MESH))

    local = []

    def bring(src, dst):
        copy = pltpu.make_async_copy(src, dst, w_sem.at[len(local)])
        copy.start()
        local.append(copy)
        return copy

    def bring_layer(l):
        g = {}
        g["qkv"] = [bring(wqkv_hbm.at[l, j], wqkv.at[l, j]) for j in range(3)]
        g["fc1"] = [bring(wfc1_hbm.at[l, :, pl.ds(ff_at, ff)], wfc1.at[l])]
        g["cache"] = [
            bring(cache_hbm.at[l, i], cache.at[l, i, pl.ds(0, slots)]) for i in range(2)]
        g["fc2"] = [bring(wfc2_hbm.at[l, pl.ds(ff_at, ff), :], wfc2.at[l])]
        g["out"] = [bring(wout_hbm.at[l], wout.at[l])]
        return g

    got = {0: bring_layer(0)}

    def remote(src, dst, ssem, rsem, peer):
        return pltpu.make_async_remote_copy(
            src_ref=src, dst_ref=dst, send_sem=ssem, recv_sem=rsem,
            device_id=peer, device_id_type=MESH)

    def copy_a(l, part):
        piece = pl.ds(2 * part, 2)
        return lambda k: remote(
            buf_a.at[l, 0, piece], buf_a.at[l, k, piece],
            a_send.at[l, k, part], a_recv.at[l, k, part], blk_peer(k))

    def copy_i(l):
        return lambda k: remote(
            buf_i.at[l, 0], buf_i.at[l, k], i_send.at[l, k], i_recv.at[l, k], blk_peer(k))

    def copy_q(l):
        return lambda k: remote(
            buf_q.at[l, 0], buf_q.at[l, k], q_send.at[l, k], q_recv.at[l, k], rep_peer(k))

    def copy_b(l):
        return lambda k: remote(
            msg.at[l, lax.rem(my_flat + k, n_all) // n_blk], buf_b.at[l, k],
            b_send.at[l, k], b_recv.at[l, k], flat_peer(k))

    def copy_x(l):
        return lambda k: remote(
            buf_x.at[l, 0], buf_x.at[l, k], x_send.at[l, k], x_recv.at[l, k], rep_peer(k))

    def copy_m(l):
        return lambda k: remote(
            msg_m.at[l, lax.rem(my_rep + k, n_rep)], buf_m.at[l, k],
            m_send.at[l, k], m_recv.at[l, k], rep_peer(k))

    def copy_c(l):
        return lambda k: remote(
            buf_c.at[l, 0], buf_c.at[l, k], c_send.at[l, k], c_recv.at[l, k], tp_peer(k))

    feature = lax.rem(lane_iota((2 * rows, width)), HD)
    small = (2 * rows, 128)
    posv = jnp.zeros(small, f32)
    for r in range(rows):
        posv = jnp.where(
            lax.rem(row_iota(small), rows) == r, pos_ref[r].astype(f32), posv)
    angles = posv * freq_ref[...]
    cosine = jnp.concatenate([jnp.cos(angles)] * (width // 128), axis=1)
    sine = jnp.concatenate([jnp.sin(angles)] * (width // 128), axis=1)
    sine = jnp.where(feature < ROT // 2, -sine, sine)

    extra = cache.shape[2] - slots
    columns = (slots + extra) * PAGE
    lanes = lane_iota((1, columns))
    col_owner = jnp.full((1, columns), -1, jnp.int32)
    home = jnp.full((slots, width), -1, jnp.int32)
    for s in range(slots):
        limit = jnp.where(used_ref[s] == 1, fill_ref[s], 0)
        here = (lanes >= s * PAGE) & (lanes < s * PAGE + limit)
        col_owner = jnp.where(here, owner_ref[s], col_owner)
        home_row = jnp.where(tail_ref[s] == 1, owner_ref[s] - my_rep * rows, -1)
        home = jnp.where(row_iota((slots, width)) == s, home_row, home)
        new_lane = jnp.where(tail_ref[s] == 1, slots * PAGE + home_row, -1)
        col_owner = jnp.where(lanes == new_lane, owner_ref[s], col_owner)
        write_pos = jnp.where(tail_ref[s] == 1, fill_ref[s], -1)
        bound_ref[s] = jnp.where(
            row_iota((PAGE, width)) == write_pos, -jnp.inf, jnp.inf).astype(bf16)
    bound_copy = pltpu.make_async_copy(bound_ref, bound_hbm, o_sem.at[0])
    bound_copy.start()
    mask_ref[...] = jnp.where(
        lax.rem(row_iota((heads * reqs, columns)), reqs) == col_owner, 1.0, 0.0)
    for l in range(LAYERS):
        for i in range(2):
            for s in range(slots, slots + extra):
                cache[l, i, s] = jnp.zeros((PAGE, width), bf16)

    head_of_lane = lane_iota((1, width)) // HD

    def expand(stat):
        out = jnp.broadcast_to(stat[:, 0:1], (stat.shape[0], width))
        for h in range(1, heads):
            out = jnp.where(head_of_lane == h, stat[:, h:h + 1], out)
        return out

    def fold(x):
        part = x.shape[1] // 4
        return jnp.concatenate([x[:, c * part:(c + 1) * part] for c in range(4)], axis=0)

    def unfold(x):
        x = x.astype(f32)
        return jnp.concatenate([x[c * rows:(c + 1) * rows] for c in range(4)], axis=1)

    def split(x):
        high = x.astype(bf16).astype(f32)
        return high, (x - high).astype(bf16).astype(f32)

    wide = model >= 512

    def fold_c(x):
        if wide:
            return fold(x)
        x = jnp.concatenate([x, jnp.zeros((16 - rows, model), f32)], axis=0)
        if model < buf_c.shape[3]:
            x = jnp.concatenate([x, jnp.zeros((16, buf_c.shape[3] - model), f32)], axis=1)
        return x

    def unfold_c(x):
        if wide:
            return unfold(x)
        return x[0:rows, 0:model]

    def fold_m(x):
        if wide:
            return jnp.concatenate([x[:, :model // 2], x[:, model // 2:]], axis=0)
        x = jnp.concatenate([x, jnp.zeros((2 * rows - rows, model), f32)], axis=0)
        if model < buf_m.shape[3]:
            x = jnp.concatenate(
                [x, jnp.zeros((2 * rows, buf_m.shape[3] - model), f32)], axis=1)
        return x

    def unfold_m(x):
        if wide:
            return jnp.concatenate([x[:rows], x[rows:]], axis=1)
        return x[0:rows, 0:model]

    def center(x):
        own_mean = jnp.sum(x, axis=1, keepdims=True) / model
        centered = x - own_mean
        return own_mean, centered, jnp.sum(centered * centered, axis=1, keepdims=True)

    def whole_norm(mean_of, square_of, count):
        blank = jnp.zeros((count, 1), f32)
        mean = fold_sum(0, n_blk, lambda k, t: t + mean_of(k), blank) / n_blk

        def add_square(k, total):
            off = mean_of(k) - mean
            return total + (square_of(k) + model * (off * off))

        square = fold_sum(0, n_blk, add_square, blank)
        return mean, lax.rsqrt(square / full_model + EPSILON)

    def sum_parts(block_of, mean_of, mean, scale, count, columns):
        def add(k, total):
            block = block_of(k)
            gained = block[count:count + 1] + block[count + 1:count + 2]
            return total + (block[0:count] + (mean_of(k) - mean) * gained)

        return fold_sum(0, n_blk, add, jnp.zeros((count, columns), f32)) * scale

    state = hidden_ref[...].astype(f32)
    for l in range(LAYERS):
        g = got[l]
        buf_x[l, 0] = fold_c(state).astype(bf16)
        if l > 0:
            each(1, n_rep, lambda k: copy_x(l)(k).start())
        own_mean, centered, own_square = center(state)
        gain = gain_ref[l:l + 1, :]
        gain_hi = gain.astype(bf16).astype(f32)
        gain_lo = gain - gain_hi
        lhs = jnp.concatenate(
            [centered * gain, gain_hi, gain_lo, jnp.zeros((2 * rows - rows - 2, model), f32)],
            axis=0).astype(bf16)
        stat_lane = lane_iota((rows, width))
        stats = jnp.where(stat_lane < 128, own_mean, own_square)
        buf_a[l, 0, 0] = jnp.concatenate([stats, jnp.zeros((rows, width), f32)], axis=0)

        def project(j):
            g["qkv"][j].wait()
            buf_a[l, 0, 1 + j] = jnp.dot(lhs, wqkv[l, j], preferred_element_type=f32)

        project(0)
        if l == 0:
            pl.semaphore_wait(barrier, n_all - 1 + n_tp - 1)
            each(1, n_rep, lambda k: copy_x(l)(k).start())
        each(1, n_blk, lambda k: copy_a(l, 0)(k).start())
        project(1)
        project(2)
        each(1, n_blk, lambda k: copy_a(l, 1)(k).start())
        each(1, n_blk, lambda k: copy_a(l, 0)(k).wait_recv())
        def mean_a(k):
            return buf_a[l, k, 0, 0:rows, 0:1]

        mean, scale = whole_norm(
            mean_a, lambda k: buf_a[l, k, 0, 0:rows, 128:129], rows)

        def finish(j):
            return sum_parts(lambda k: buf_a[l, k, j], mean_a, mean, scale, rows, width)

        def rotate(x):
            turned = jnp.where(
                feature < ROT // 2,
                pltpu.roll(x, width - ROT // 2, 1),
                pltpu.roll(x, ROT // 2, 1))
            return (x * cosine + turned * sine).astype(bf16).astype(f32)

        blank = jnp.zeros((rows, width), f32)
        own_queries = rotate(jnp.concatenate([finish(1), blank], axis=0))[:rows]
        buf_q[l, 0] = fold(own_queries).astype(bf16)
        each(1, n_rep, lambda k: copy_q(l)(k).start())

        each(1, n_rep, lambda k: copy_x(l)(k).wait_recv())
        all_state = jnp.concatenate(
            [unfold_c(buf_x[l, lax.rem(my_rep - t + n_rep, n_rep)].astype(f32))
             for t in range(n_rep)], axis=0)
        all_mean, all_centered, all_square = center(all_state)
        all_lhs = jnp.concatenate(
            [all_centered * gain, gain_hi, gain_lo, jnp.zeros((6, model), f32)],
            axis=0).astype(bf16)
        all_stats = jnp.where(lane_iota((reqs, 128)) < 64, all_mean, all_square)
        buf_i[l, 0, :, ff:ff + 128] = jnp.concatenate(
            [all_stats, jnp.zeros((8, 128), f32)], axis=0)
        g["fc1"][0].wait()
        buf_i[l, 0, :, 0:ff] = jnp.dot(all_lhs, wfc1[l], preferred_element_type=f32)
        each(1, n_blk, lambda k: copy_i(l)(k).start())
        if l + 1 < LAYERS:
            got[l + 1] = bring_layer(l + 1)
        each(1, n_blk, lambda k: copy_a(l, 1)(k).wait_recv())
        new_k = rotate(jnp.concatenate([finish(2), blank], axis=0))[:rows]
        new_v = finish(3).astype(bf16).astype(f32)
        new = (new_k, new_v)
        for i in range(2):
            cache[l, i, slots, 0:16] = jnp.concatenate(
                [new[i], jnp.zeros((16 - rows, width), f32)], axis=0).astype(bf16)

        each(1, n_blk, lambda k: copy_i(l)(k).wait_recv())

        def mean_i(k):
            return buf_i[l, k, 0:reqs, ff:ff + 1]

        mean, scale = whole_norm(
            mean_i, lambda k: buf_i[l, k, 0:reqs, ff + 64:ff + 65], reqs)
        inner = sum_parts(lambda k: buf_i[l, k, :, 0:ff], mean_i, mean, scale, reqs, ff)
        act = jax.nn.gelu(inner, approximate=True).astype(bf16)
        g["fc2"][0].wait()
        mlp_all = jnp.dot(act, wfc2[l], preferred_element_type=f32)
        for r in range(n_rep):
            msg_m[l, r] = fold_m(mlp_all[r * rows:(r + 1) * rows])
        each(1, n_rep, lambda k: copy_m(l)(k).start())

        each(1, n_rep, lambda k: copy_q(l)(k).wait_recv())
        queries = jnp.concatenate(
            [unfold(buf_q[l, lax.rem(my_rep - t + n_rep, n_rep)]) for t in range(n_rep)], axis=0)
        by_head = jnp.concatenate(
            [jnp.where(head_of_lane == h, queries, 0.0) for h in range(heads)], axis=0
        ).astype(bf16)
        for i in range(2):
            g["cache"][i].wait()
        keys = cache[l, 0].reshape(columns, width)
        values = cache[l, 1].reshape(columns, width)
        scores = lax.dot_general(
            by_head, keys, (((1,), (1,)), ((), ())), preferred_element_type=f32) * HD ** (-0.5)
        mask = mask_ref[...] > 0.0
        scores = jnp.where(mask, scores, LOWEST)
        high_pieces = split(jnp.max(scores, axis=1, keepdims=True))
        highest = high_pieces[0] + high_pieces[1]
        weights = jnp.where(mask, jnp.exp(scores - highest), 0.0)
        totals = jnp.sum(weights, axis=1, keepdims=True)
        spread = jnp.dot(weights.astype(bf16), values, preferred_element_type=f32)
        out = spread[0:reqs]
        stat_shape = (reqs, 128)
        stats = [jnp.zeros(stat_shape, f32), jnp.zeros(stat_shape, f32),
                 jnp.ones(stat_shape, f32), jnp.zeros(stat_shape, f32)]
        for h in range(heads):
            part = slice(h * reqs, (h + 1) * reqs)
            if h > 0:
                out = jnp.where(head_of_lane == h, spread[part], out)
            for i, piece in enumerate(high_pieces + split(totals)):
                stats[i] = jnp.where(lane_iota(stat_shape) == h, piece[part], stats[i])
        for r in range(n_rep):
            part = slice(r * rows, (r + 1) * rows)
            msg[l, r] = jnp.concatenate(
                [fold(out[part]), jnp.concatenate([stat[part] for stat in stats], axis=0)],
                axis=1).astype(bf16)
        each(1, n_all, lambda k: copy_b(l)(k).start())
        buf_b[l, 0] = msg[l, my_rep]

        each(1, n_rep, lambda k: copy_m(l)(k).wait_recv())
        mlp = fold_sum(1, n_rep, lambda k, t: t + buf_m[l, k], msg_m[l, my_rep])

        each(1, n_all, lambda k: copy_b(l)(k).wait_recv())

        def stat_of(k, first):
            stat = buf_b[l, k, :, quarter:quarter + 128].astype(f32)
            return stat[first * rows:(first + 1) * rows] + stat[(first + 1) * rows:(first + 2) * rows]

        top = fold_sum(
            0, n_all, lambda k, t: jnp.maximum(t, stat_of(k, 0)),
            jnp.full((rows, 128), LOWEST, f32))

        def merge(k, carry):
            denom, numer = carry
            factor = jnp.exp(stat_of(k, 0) - top)
            denom = denom + factor * stat_of(k, 2)
            numer = numer + expand(factor) * unfold(buf_b[l, k, :, 0:quarter])
            return denom, numer

        denom, numer = fold_sum(
            0, n_all, merge, (jnp.zeros((rows, 128), f32), jnp.zeros((rows, width), f32)))
        attended = numer / expand(denom)
        attended = jnp.concatenate(
            [attended, jnp.zeros((rows, width), f32)], axis=0).astype(bf16)
        g["out"][0].wait()
        branch = (
            jnp.dot(attended, wout[l], preferred_element_type=f32)[0:rows] + unfold_m(mlp))
        buf_c[l, 0] = fold_c(branch).astype(bf16)
        each(1, n_tp, lambda k: copy_c(l)(k).start())

        for i in range(2):
            fresh = jnp.zeros((slots, width), f32)
            for r in range(rows):
                fresh = jnp.where(home == r, new[i][r:r + 1], fresh)
            fresh_ref[l, i] = fresh.astype(bf16)

        each(1, n_tp, lambda k: copy_c(l)(k).wait_recv())
        total = buf_c[l, lax.rem(my_tp + n_tp, n_tp)].astype(f32)
        for t in range(1, n_tp):
            total = total + buf_c[l, lax.rem(my_tp - t + n_tp, n_tp)].astype(f32)
        total = unfold_c(total)
        state = (state + total).astype(bf16).astype(f32)

    state_ref[...] = state
    bound_copy.wait()
    for l in range(LAYERS):
        each(1, n_blk, lambda k: copy_a(l, 0)(k).wait_send())
        each(1, n_blk, lambda k: copy_a(l, 1)(k).wait_send())
        each(1, n_blk, lambda k: copy_i(l)(k).wait_send())
        each(1, n_rep, lambda k: copy_q(l)(k).wait_send())
        each(1, n_rep, lambda k: copy_x(l)(k).wait_send())
        each(1, n_rep, lambda k: copy_m(l)(k).wait_send())
        each(1, n_all, lambda k: copy_b(l)(k).wait_send())
        each(1, n_tp, lambda k: copy_c(l)(k).wait_send())


def frequencies(rows):
    feature = np.arange(128) % HD
    power = 10000.0 ** (-2.0 * (feature % (ROT // 2)) / ROT)
    return np.tile(np.where(feature < ROT, power, 0.0).astype(np.float32)[None, :], (rows, 1))


def per_device(
    hidden, ln_gain, w_qkv, w_fc1, w_out, w_fc2, caches,
    page_owner, page_used, page_fill, page_tail, positions,
):
    n_rep, n_blk, n_tp = (lax.axis_size(a) for a in ("rep", "blk", "tp"))
    f32, bf16 = jnp.float32, jnp.bfloat16
    rows, model = hidden.shape
    slots = page_owner.shape[0]
    width = w_out.shape[1]
    ff = w_fc1.shape[2] // n_rep
    n_all = n_rep * n_blk
    wq = jnp.transpose(w_qkv, (0, 2, 1, 3))
    c_width = model // 4 if model >= 512 else max(model, 128)
    m_width = model // 2 if model >= 512 else max(model, 128)
    extra = 128 // PAGE
    smem = pl.BlockSpec(memory_space=pltpu.SMEM)
    vmem = pl.BlockSpec(memory_space=pltpu.VMEM)
    anywhere = pl.BlockSpec(memory_space=pl.ANY)
    dma = pltpu.SemaphoreType.DMA
    n_copies = LAYERS * (3 + 1 + 2 + 1 + 1)
    state, fresh, bound = pl.pallas_call(
        functools.partial(kernel, n_rep, n_blk, n_tp),
        out_shape=(
            jax.ShapeDtypeStruct((rows, model), f32),
            jax.ShapeDtypeStruct((LAYERS, 2, slots, width), bf16),
            jax.ShapeDtypeStruct((slots, PAGE, width), bf16),
        ),
        in_specs=[smem] * 5 + [vmem] * 3 + [anywhere] * 5,
        out_specs=(vmem, vmem, anywhere),
        scratch_shapes=[
            pltpu.VMEM((LAYERS, 3, model, width), bf16),
            pltpu.VMEM((LAYERS, model, ff), bf16),
            pltpu.VMEM((LAYERS, width, model), bf16),
            pltpu.VMEM((LAYERS, ff, model), bf16),
            pltpu.VMEM((LAYERS, 2, slots + extra, PAGE, width), bf16),
            pltpu.VMEM((LAYERS, n_blk, 4, 2 * rows, width), f32),
            pltpu.VMEM((LAYERS, n_blk, rows * n_rep + 8, ff + 128), f32),
            pltpu.VMEM((LAYERS, n_rep, 4 * rows, width // 4), bf16),
            pltpu.VMEM((LAYERS, n_rep, 4 * rows, width // 4 + 128), bf16),
            pltpu.VMEM((LAYERS, n_all, 4 * rows, width // 4 + 128), bf16),
            pltpu.VMEM((LAYERS, n_tp, 16, c_width), bf16),
            pltpu.VMEM((LAYERS, n_rep, 16, c_width), bf16),
            pltpu.VMEM((LAYERS, n_rep, 2 * rows, m_width), f32),
            pltpu.VMEM((LAYERS, n_rep, 2 * rows, m_width), f32),
            pltpu.VMEM((width // HD * rows * n_rep, (slots + extra) * PAGE), f32),
            pltpu.VMEM((slots, PAGE, width), bf16),
            dma((n_copies,)), dma((1,)),
            dma((LAYERS, n_blk, 2)), dma((LAYERS, n_blk, 2)),
            dma((LAYERS, n_blk)), dma((LAYERS, n_blk)),
            dma((LAYERS, n_rep)), dma((LAYERS, n_rep)),
            dma((LAYERS, n_all)), dma((LAYERS, n_all)),
            dma((LAYERS, n_tp)), dma((LAYERS, n_tp)),
            dma((LAYERS, n_rep)), dma((LAYERS, n_rep)),
            dma((LAYERS, n_rep)), dma((LAYERS, n_rep)),
        ],
        compiler_params=pltpu.CompilerParams(
            collective_id=0, has_side_effects=True, vmem_limit_bytes=56 * 2**20),
        name="decode_layers",
    )(
        page_owner, page_used, page_fill, page_tail, positions,
        hidden, ln_gain, jnp.asarray(frequencies(2 * rows)),
        wq, w_fc1, w_out, w_fc2, caches,
    )
    caches_out = jnp.where(caches < bound[None, None], caches, fresh[:, :, :, None, :])
    return (state.astype(bf16), caches_out)


def solution(mesh):
    in_specs = (
        P("rep", "blk"),
        P(None, "blk"),
        P(None, "blk", None, "tp"),
        P(None, "blk", "tp"),
        P(None, "tp", "blk"),
        P(None, "tp", "blk"),
        P(None, None, ("rep", "blk"), None, "tp"),
        P(("rep", "blk")),
        P(("rep", "blk")),
        P(("rep", "blk")),
        P(("rep", "blk")),
        P("rep"),
    )
    out_specs = (P("rep", "blk"), P(None, None, ("rep", "blk"), None, "tp"))
    return jax.shard_map(
        per_device, mesh=mesh, in_specs=in_specs, out_specs=out_specs, check_vma=False
    )
```

```python
import functools

import jax
import jax.numpy as jnp
import numpy as np
from jax import lax
from jax.experimental import pallas as pl
from jax.experimental.pallas import tpu as pltpu
from jax.sharding import PartitionSpec as P

HD = 64
ROT = 32
LAYERS = 2
PAGE = 32
EPSILON = 1e-05
LOWEST = -1e30
MESH = pl.DeviceIdType.MESH
UNROLL = 8


def each(start, stop, body):
    if stop - start <= UNROLL:
        for k in range(start, stop):
            body(k)
    else:
        lax.fori_loop(start, stop, lambda k, c: (body(k), c)[1], 0)


def fold_sum(start, stop, body, carry):
    if stop - start <= UNROLL:
        for k in range(start, stop):
            carry = body(k, carry)
        return carry
    return lax.fori_loop(start, stop, body, carry)


def lane_iota(shape):
    return lax.broadcasted_iota(jnp.int32, shape, len(shape) - 1)


def row_iota(shape):
    return lax.broadcasted_iota(jnp.int32, shape, len(shape) - 2)


def kernel(
    n_rep, n_blk, n_tp,
    owner_ref, used_ref, fill_ref, tail_ref, pos_ref,
    hidden_ref, gain_ref, freq_ref,
    wqkv_hbm, wfc1_hbm, wout_hbm, wfc2_hbm, cache_hbm,
    state_ref, fresh_ref,
    wqkv, wfc1, wout, wfc2, cache,
    buf_a, buf_i, buf_q, msg, buf_b, buf_c, mlp_acc, act_ref, mask_ref,
    w_sem, a_send, a_recv, i_send, i_recv, q_send, q_recv, b_send, b_recv, c_send, c_recv,
):
    f32, bf16 = jnp.float32, jnp.bfloat16
    rows, model = hidden_ref.shape
    full_model = model * n_blk
    slots = owner_ref.shape[0]
    width = wout.shape[1]
    heads = width // HD
    n_ff = wfc1.shape[2] // width
    reqs = rows * n_rep
    n_all = n_rep * n_blk
    quarter = width // 4
    my_rep, my_blk, my_tp = lax.axis_index("rep"), lax.axis_index("blk"), lax.axis_index("tp")
    my_flat = my_rep * n_blk + my_blk
    ff_half = n_ff // 2

    def flat_peer(k):
        to = lax.rem(my_flat + k, n_all)
        return {"rep": to // n_blk, "blk": lax.rem(to, n_blk)}

    def blk_peer(k):
        return {"blk": lax.rem(my_blk + k, n_blk)}

    def rep_peer(k):
        return {"rep": lax.rem(my_rep + k, n_rep)}

    def tp_peer(k):
        return {"tp": lax.rem(my_tp + k, n_tp)}

    barrier = pltpu.get_barrier_semaphore()
    each(1, n_all, lambda k: pl.semaphore_signal(
        barrier, inc=1, device_id=flat_peer(k), device_id_type=MESH))
    each(1, n_tp, lambda k: pl.semaphore_signal(
        barrier, inc=1, device_id=tp_peer(k), device_id_type=MESH))

    local = []

    def bring(src, dst):
        copy = pltpu.make_async_copy(src, dst, w_sem.at[len(local)])
        copy.start()
        local.append(copy)
        return copy

    def bring_layer(l, pieces):
        g = {}
        g["qkv"] = [bring(wqkv_hbm.at[l, j], wqkv.at[l, j]) for j in range(3)]
        step = n_ff // pieces
        g["fc1"] = [
            bring(wfc1_hbm.at[l, :, pl.ds(c * width, step * width)],
                  wfc1.at[l, :, pl.ds(c * width, step * width)])
            if c % step == 0 else None for c in range(n_ff)
        ]
        g["cache"] = [
            bring(cache_hbm.at[l, i], cache.at[l, i, pl.ds(0, slots)]) for i in range(2)]
        g["fc2"] = [
            bring(wfc2_hbm.at[l, pl.ds(i * ff_half * width, ff_half * width), :], wfc2.at[l, i])
            for i in range(2)
        ]
        g["out"] = [bring(wout_hbm.at[l], wout.at[l])]
        return g

    got = {0: bring_layer(0, n_ff // 2)}

    def remote(src, dst, ssem, rsem, peer):
        return pltpu.make_async_remote_copy(
            src_ref=src, dst_ref=dst, send_sem=ssem, recv_sem=rsem,
            device_id=peer, device_id_type=MESH)

    def copy_a(l, part):
        piece = pl.ds(2 * part, 2)
        return lambda k: remote(
            buf_a.at[l, 0, piece], buf_a.at[l, k, piece],
            a_send.at[l, k, part], a_recv.at[l, k, part], blk_peer(k))

    def copy_i(l):
        return lambda k: remote(
            buf_i.at[l, 0], buf_i.at[l, k], i_send.at[l, k], i_recv.at[l, k], blk_peer(k))

    def copy_q(l):
        return lambda k: remote(
            buf_q.at[l, 0], buf_q.at[l, k], q_send.at[l, k], q_recv.at[l, k], rep_peer(k))

    def copy_b(l):
        return lambda k: remote(
            msg.at[l, lax.rem(my_flat + k, n_all) // n_blk], buf_b.at[l, k],
            b_send.at[l, k], b_recv.at[l, k], flat_peer(k))

    def copy_c(l):
        return lambda k: remote(
            buf_c.at[l, 0], buf_c.at[l, k], c_send.at[l, k], c_recv.at[l, k], tp_peer(k))

    feature = lax.rem(lane_iota((2 * rows, width)), HD)
    small = (2 * rows, 128)
    posv = jnp.zeros(small, f32)
    for r in range(rows):
        posv = jnp.where(
            lax.rem(row_iota(small), rows) == r, pos_ref[r].astype(f32), posv)
    angles = posv * freq_ref[...]
    cosine = jnp.concatenate([jnp.cos(angles)] * (width // 128), axis=1)
    sine = jnp.concatenate([jnp.sin(angles)] * (width // 128), axis=1)
    sine = jnp.where(feature < ROT // 2, -sine, sine)

    extra = cache.shape[2] - slots
    columns = (slots + extra) * PAGE
    lanes = lane_iota((1, columns))
    col_owner = jnp.full((1, columns), -1, jnp.int32)
    home = jnp.full((slots, width), -1, jnp.int32)
    for s in range(slots):
        limit = jnp.where(used_ref[s] == 1, fill_ref[s], 0)
        here = (lanes >= s * PAGE) & (lanes < s * PAGE + limit)
        col_owner = jnp.where(here, owner_ref[s], col_owner)
        home_row = jnp.where(tail_ref[s] == 1, owner_ref[s] - my_rep * rows, -1)
        home = jnp.where(row_iota((slots, width)) == s, home_row, home)
        new_lane = jnp.where(tail_ref[s] == 1, slots * PAGE + home_row, -1)
        col_owner = jnp.where(lanes == new_lane, owner_ref[s], col_owner)
    mask_ref[...] = jnp.where(
        lax.rem(row_iota((heads * reqs, columns)), reqs) == col_owner, 1.0, 0.0)
    for l in range(LAYERS):
        for i in range(2):
            for s in range(slots, slots + extra):
                cache[l, i, s] = jnp.zeros((PAGE, width), bf16)

    head_of_lane = lane_iota((1, width)) // HD

    def expand(stat):
        out = jnp.broadcast_to(stat[:, 0:1], (stat.shape[0], width))
        for h in range(1, heads):
            out = jnp.where(head_of_lane == h, stat[:, h:h + 1], out)
        return out

    def fold(x):
        part = x.shape[1] // 4
        return jnp.concatenate([x[:, c * part:(c + 1) * part] for c in range(4)], axis=0)

    def unfold(x):
        x = x.astype(f32)
        return jnp.concatenate([x[c * rows:(c + 1) * rows] for c in range(4)], axis=1)

    def split(x):
        high = x.astype(bf16).astype(f32)
        return high, (x - high).astype(bf16).astype(f32)

    wide = model >= 512

    def fold_c(x):
        if wide:
            return fold(x)
        x = jnp.concatenate([x, jnp.zeros((16 - rows, model), f32)], axis=0)
        if model < buf_c.shape[3]:
            x = jnp.concatenate([x, jnp.zeros((16, buf_c.shape[3] - model), f32)], axis=1)
        return x

    def unfold_c(x):
        if wide:
            return unfold(x)
        return x[0:rows, 0:model]

    state = hidden_ref[...].astype(f32)
    for l in range(LAYERS):
        g = got[l]
        own_mean = jnp.sum(state, axis=1, keepdims=True) / model
        centered = state - own_mean
        own_square = jnp.sum(centered * centered, axis=1, keepdims=True)
        gain = gain_ref[l:l + 1, :]
        gain_hi = gain.astype(bf16).astype(f32)
        gain_lo = gain - gain_hi
        lhs = jnp.concatenate(
            [centered * gain, gain_hi, gain_lo, jnp.zeros((2 * rows - rows - 2, model), f32)],
            axis=0).astype(bf16)
        stat_lane = lane_iota((rows, width))
        stats = jnp.where(stat_lane < 128, own_mean, own_square)
        buf_a[l, 0, 0] = jnp.concatenate([stats, jnp.zeros((rows, width), f32)], axis=0)

        def project(j):
            g["qkv"][j].wait()
            buf_a[l, 0, 1 + j] = jnp.dot(lhs, wqkv[l, j], preferred_element_type=f32)

        def project_ff(c):
            if g["fc1"][c] is not None:
                g["fc1"][c].wait()
            buf_i[l, 0, c] = jnp.dot(
                lhs, wfc1[l, :, c * width:(c + 1) * width], preferred_element_type=f32)

        project(0)
        if l == 0:
            pl.semaphore_wait(barrier, n_all - 1 + n_tp - 1)
        each(1, n_blk, lambda k: copy_a(l, 0)(k).start())
        project(1)
        project(2)
        each(1, n_blk, lambda k: copy_a(l, 1)(k).start())
        for c in range(ff_half):
            project_ff(c)

        each(1, n_blk, lambda k: copy_a(l, 0)(k).wait_recv())
        mean = fold_sum(0, n_blk, lambda k, t: t + buf_a[l, k, 0, 0:rows, 0:1],
                        jnp.zeros((rows, 1), f32)) / n_blk

        def add_square(k, total):
            off = buf_a[l, k, 0, 0:rows, 0:1] - mean
            return total + (buf_a[l, k, 0, 0:rows, 128:129] + model * (off * off))

        square = fold_sum(0, n_blk, add_square, jnp.zeros((rows, 1), f32))
        scale = lax.rsqrt(square / full_model + EPSILON)

        def finish(buf, j):
            def add(k, total):
                off = buf_a[l, k, 0, 0:rows, 0:1] - mean
                block = buf[l, k, j]
                gained = block[rows:rows + 1] + block[rows + 1:rows + 2]
                return total + (block[0:rows] + off * gained)

            return fold_sum(0, n_blk, add, jnp.zeros((rows, width), f32)) * scale

        def rotate(x):
            turned = jnp.where(
                feature < ROT // 2,
                pltpu.roll(x, width - ROT // 2, 1),
                pltpu.roll(x, ROT // 2, 1))
            return (x * cosine + turned * sine).astype(bf16).astype(f32)

        blank = jnp.zeros((rows, width), f32)
        own_queries = rotate(jnp.concatenate([finish(buf_a, 1), blank], axis=0))[:rows]
        buf_q[l, 0] = fold(own_queries).astype(bf16)
        each(1, n_rep, lambda k: copy_q(l)(k).start())
        for c in range(ff_half, n_ff):
            project_ff(c)
        each(1, n_blk, lambda k: copy_i(l)(k).start())
        if l + 1 < LAYERS:
            got[l + 1] = bring_layer(l + 1, 1)
        each(1, n_blk, lambda k: copy_a(l, 1)(k).wait_recv())
        new_k = rotate(jnp.concatenate([finish(buf_a, 2), blank], axis=0))[:rows]
        new_v = finish(buf_a, 3).astype(bf16).astype(f32)
        new = (new_k, new_v)
        for i in range(2):
            cache[l, i, slots, 0:16] = jnp.concatenate(
                [new[i], jnp.zeros((16 - rows, width), f32)], axis=0).astype(bf16)

        each(1, n_blk, lambda k: copy_i(l)(k).wait_recv())
        for c in range(n_ff):
            act = jax.nn.gelu(finish(buf_i, c), approximate=True)
            act_ref[c] = jnp.concatenate([act, jnp.zeros((rows, width), f32)], axis=0).astype(bf16)
        g["fc2"][0].wait()
        mlp_acc[...] = jnp.dot(
            jnp.concatenate([act_ref[c] for c in range(ff_half)], axis=1),
            wfc2[l, 0], preferred_element_type=f32)

        each(1, n_rep, lambda k: copy_q(l)(k).wait_recv())
        queries = jnp.concatenate(
            [unfold(buf_q[l, lax.rem(my_rep - t + n_rep, n_rep)]) for t in range(n_rep)], axis=0)
        by_head = jnp.concatenate(
            [jnp.where(head_of_lane == h, queries, 0.0) for h in range(heads)], axis=0
        ).astype(bf16)
        for i in range(2):
            g["cache"][i].wait()
        keys = cache[l, 0].reshape(columns, width)
        values = cache[l, 1].reshape(columns, width)
        scores = lax.dot_general(
            by_head, keys, (((1,), (1,)), ((), ())), preferred_element_type=f32) * HD ** (-0.5)
        mask = mask_ref[...] > 0.0
        scores = jnp.where(mask, scores, LOWEST)
        high_pieces = split(jnp.max(scores, axis=1, keepdims=True))
        highest = high_pieces[0] + high_pieces[1]
        weights = jnp.where(mask, jnp.exp(scores - highest), 0.0)
        totals = jnp.sum(weights, axis=1, keepdims=True)
        spread = jnp.dot(weights.astype(bf16), values, preferred_element_type=f32)
        out = spread[0:reqs]
        stat_shape = (reqs, 128)
        stats = [jnp.zeros(stat_shape, f32), jnp.zeros(stat_shape, f32),
                 jnp.ones(stat_shape, f32), jnp.zeros(stat_shape, f32)]
        for h in range(heads):
            part = slice(h * reqs, (h + 1) * reqs)
            if h > 0:
                out = jnp.where(head_of_lane == h, spread[part], out)
            for i, piece in enumerate(high_pieces + split(totals)):
                stats[i] = jnp.where(lane_iota(stat_shape) == h, piece[part], stats[i])
        for r in range(n_rep):
            part = slice(r * rows, (r + 1) * rows)
            msg[l, r] = jnp.concatenate(
                [fold(out[part]), jnp.concatenate([stat[part] for stat in stats], axis=0)],
                axis=1).astype(bf16)
        each(1, n_all, lambda k: copy_b(l)(k).start())
        buf_b[l, 0] = msg[l, my_rep]

        g["fc2"][1].wait()
        mlp_acc[...] += jnp.dot(
            jnp.concatenate([act_ref[c] for c in range(ff_half, n_ff)], axis=1),
            wfc2[l, 1], preferred_element_type=f32)

        each(1, n_all, lambda k: copy_b(l)(k).wait_recv())

        def stat_of(k, first):
            stat = buf_b[l, k, :, quarter:quarter + 128].astype(f32)
            return stat[first * rows:(first + 1) * rows] + stat[(first + 1) * rows:(first + 2) * rows]

        top = fold_sum(
            0, n_all, lambda k, t: jnp.maximum(t, stat_of(k, 0)),
            jnp.full((rows, 128), LOWEST, f32))

        def merge(k, carry):
            denom, numer = carry
            factor = jnp.exp(stat_of(k, 0) - top)
            denom = denom + factor * stat_of(k, 2)
            numer = numer + expand(factor) * unfold(buf_b[l, k, :, 0:quarter])
            return denom, numer

        denom, numer = fold_sum(
            0, n_all, merge, (jnp.zeros((rows, 128), f32), jnp.zeros((rows, width), f32)))
        attended = numer / expand(denom)
        attended = jnp.concatenate(
            [attended, jnp.zeros((rows, width), f32)], axis=0).astype(bf16)
        g["out"][0].wait()
        branch = (
            jnp.dot(attended, wout[l], preferred_element_type=f32) + mlp_acc[...])[0:rows]
        buf_c[l, 0] = fold_c(branch).astype(bf16)
        each(1, n_tp, lambda k: copy_c(l)(k).start())

        for i in range(2):
            fresh = jnp.zeros((slots, width), f32)
            for r in range(rows):
                fresh = jnp.where(home == r, new[i][r:r + 1], fresh)
            fresh_ref[l, i] = fresh.astype(bf16)

        each(1, n_blk, lambda k: copy_a(l, 0)(k).wait_send())
        each(1, n_blk, lambda k: copy_a(l, 1)(k).wait_send())
        each(1, n_blk, lambda k: copy_i(l)(k).wait_send())
        each(1, n_rep, lambda k: copy_q(l)(k).wait_send())
        each(1, n_all, lambda k: copy_b(l)(k).wait_send())

        each(1, n_tp, lambda k: copy_c(l)(k).wait_recv())
        total = buf_c[l, lax.rem(my_tp + n_tp, n_tp)].astype(f32)
        for t in range(1, n_tp):
            total = total + buf_c[l, lax.rem(my_tp - t + n_tp, n_tp)].astype(f32)
        total = unfold_c(total)
        state = (state + total).astype(bf16).astype(f32)

    state_ref[...] = state
    for l in range(LAYERS):
        each(1, n_tp, lambda k: copy_c(l)(k).wait_send())


def page_kernel(fill_ref, tail_ref, state_in, fresh_ref, cache_ref, state_ref, out_ref):
    page_shape = cache_ref.shape[3:]
    state_ref[...] = state_in[...].astype(state_ref.dtype)
    for s in range(cache_ref.shape[2]):
        write_pos = jnp.where(tail_ref[s] == 1, fill_ref[s], -1)
        page = cache_ref[0, 0, s].astype(jnp.float32)
        fresh = fresh_ref[0, 0, s:s + 1].astype(jnp.float32)
        out_ref[0, 0, s] = jnp.where(
            row_iota(page_shape) == write_pos, fresh, page).astype(out_ref.dtype)


def frequencies(rows):
    feature = np.arange(128) % HD
    power = 10000.0 ** (-2.0 * (feature % (ROT // 2)) / ROT)
    return np.tile(np.where(feature < ROT, power, 0.0).astype(np.float32)[None, :], (rows, 1))


def per_device(
    hidden, ln_gain, w_qkv, w_fc1, w_out, w_fc2, caches,
    page_owner, page_used, page_fill, page_tail, positions,
):
    n_rep, n_blk, n_tp = (lax.axis_size(a) for a in ("rep", "blk", "tp"))
    f32, bf16 = jnp.float32, jnp.bfloat16
    rows, model = hidden.shape
    slots = page_owner.shape[0]
    width = w_out.shape[1]
    n_ff = w_fc1.shape[2] // width
    n_all = n_rep * n_blk
    wq = jnp.transpose(w_qkv, (0, 2, 1, 3))
    c_width = model // 4 if model >= 512 else max(model, 128)
    extra = 128 // PAGE
    smem = pl.BlockSpec(memory_space=pltpu.SMEM)
    vmem = pl.BlockSpec(memory_space=pltpu.VMEM)
    anywhere = pl.BlockSpec(memory_space=pl.ANY)
    dma = pltpu.SemaphoreType.DMA
    n_copies = LAYERS * (3 + n_ff + 2 + 2 + 1)
    state, fresh = pl.pallas_call(
        functools.partial(kernel, n_rep, n_blk, n_tp),
        out_shape=(
            jax.ShapeDtypeStruct((rows, model), f32),
            jax.ShapeDtypeStruct((LAYERS, 2, slots, width), bf16),
        ),
        in_specs=[smem] * 5 + [vmem] * 3 + [anywhere] * 5,
        out_specs=(vmem, vmem),
        scratch_shapes=[
            pltpu.VMEM((LAYERS, 3, model, width), bf16),
            pltpu.VMEM((LAYERS, model, n_ff * width), bf16),
            pltpu.VMEM((LAYERS, width, model), bf16),
            pltpu.VMEM((LAYERS, 2, n_ff // 2 * width, model), bf16),
            pltpu.VMEM((LAYERS, 2, slots + extra, PAGE, width), bf16),
            pltpu.VMEM((LAYERS, n_blk, 4, 2 * rows, width), f32),
            pltpu.VMEM((LAYERS, n_blk, n_ff, 2 * rows, width), f32),
            pltpu.VMEM((LAYERS, n_rep, 4 * rows, width // 4), bf16),
            pltpu.VMEM((LAYERS, n_rep, 4 * rows, width // 4 + 128), bf16),
            pltpu.VMEM((LAYERS, n_all, 4 * rows, width // 4 + 128), bf16),
            pltpu.VMEM((LAYERS, n_tp, 16, c_width), bf16),
            pltpu.VMEM((2 * rows, model), f32),
            pltpu.VMEM((n_ff, 2 * rows, width), bf16),
            pltpu.VMEM((width // HD * rows * n_rep, (slots + extra) * PAGE), f32),
            dma((n_copies,)),
            dma((LAYERS, n_blk, 2)), dma((LAYERS, n_blk, 2)),
            dma((LAYERS, n_blk)), dma((LAYERS, n_blk)),
            dma((LAYERS, n_rep)), dma((LAYERS, n_rep)),
            dma((LAYERS, n_all)), dma((LAYERS, n_all)),
            dma((LAYERS, n_tp)), dma((LAYERS, n_tp)),
        ],
        compiler_params=pltpu.CompilerParams(
            collective_id=0, has_side_effects=True, vmem_limit_bytes=56 * 2**20),
        name="decode_layers",
    )(
        page_owner, page_used, page_fill, page_tail, positions,
        hidden, ln_gain, jnp.asarray(frequencies(2 * rows)),
        wq, w_fc1, w_out, w_fc2, caches,
    )
    block = pl.BlockSpec(
        (1, 1, slots, PAGE, width), lambda l, i: (l, i, 0, 0, 0))
    return pl.pallas_call(
        page_kernel,
        grid=(LAYERS, 2),
        out_shape=(
            jax.ShapeDtypeStruct((rows, model), bf16),
            jax.ShapeDtypeStruct(caches.shape, bf16),
        ),
        in_specs=[
            smem, smem,
            pl.BlockSpec((rows, model), lambda l, i: (0, 0)),
            pl.BlockSpec((1, 1, slots, width), lambda l, i: (l, i, 0, 0)),
            block,
        ],
        out_specs=(pl.BlockSpec((rows, model), lambda l, i: (0, 0)), block),
        name="write_pages",
    )(page_fill, page_tail, state, fresh, caches)


def solution(mesh):
    in_specs = (
        P("rep", "blk"),
        P(None, "blk"),
        P(None, "blk", None, "tp"),
        P(None, "blk", "tp"),
        P(None, "tp", "blk"),
        P(None, "tp", "blk"),
        P(None, None, ("rep", "blk"), None, "tp"),
        P(("rep", "blk")),
        P(("rep", "blk")),
        P(("rep", "blk")),
        P(("rep", "blk")),
        P("rep"),
    )
    out_specs = (P("rep", "blk"), P(None, None, ("rep", "blk"), None, "tp"))
    return jax.shard_map(
        per_device, mesh=mesh, in_specs=in_specs, out_specs=out_specs, check_vma=False
    )
```

```python
import functools

import jax
import jax.numpy as jnp
import numpy as np
from jax import lax
from jax.experimental import pallas as pl
from jax.experimental.pallas import tpu as pltpu
from jax.sharding import PartitionSpec as P

HD = 64
ROT = 32
LAYERS = 2
PAGE = 32
EPSILON = 1e-05
LOWEST = -1e30
MESH = pl.DeviceIdType.MESH
UNROLL = 8


def each(start, stop, body):
    if stop - start <= UNROLL:
        for k in range(start, stop):
            body(k)
    else:
        lax.fori_loop(start, stop, lambda k, c: (body(k), c)[1], 0)


def fold_sum(start, stop, body, carry):
    if stop - start <= UNROLL:
        for k in range(start, stop):
            carry = body(k, carry)
        return carry
    return lax.fori_loop(start, stop, body, carry)


def lane_iota(shape):
    return lax.broadcasted_iota(jnp.int32, shape, len(shape) - 1)


def row_iota(shape):
    return lax.broadcasted_iota(jnp.int32, shape, len(shape) - 2)


def kernel(
    n_rep, n_blk, n_tp,
    owner_ref, used_ref, fill_ref, tail_ref, pos_ref,
    hidden_ref, gain_ref, freq_ref,
    wqkv_hbm, wfc1_hbm, wout_hbm, wfc2_hbm, cache_hbm,
    state_ref, fresh_ref, bound_ref,
    wqkv, wfc1, wout, wfc2, cache,
    buf_a, buf_i, buf_q, msg, buf_b, buf_c, mlp_acc, act_ref, mask_ref,
    w_sem, a_send, a_recv, i_send, i_recv, q_send, q_recv, b_send, b_recv, c_send, c_recv,
):
    f32, bf16 = jnp.float32, jnp.bfloat16
    rows, model = hidden_ref.shape
    full_model = model * n_blk
    slots = owner_ref.shape[0]
    width = wout.shape[1]
    heads = width // HD
    n_ff = wfc1.shape[2] // width
    reqs = rows * n_rep
    n_all = n_rep * n_blk
    quarter = width // 4
    my_rep, my_blk, my_tp = lax.axis_index("rep"), lax.axis_index("blk"), lax.axis_index("tp")
    my_flat = my_rep * n_blk + my_blk
    ff_half = n_ff // 2

    def flat_peer(k):
        to = lax.rem(my_flat + k, n_all)
        return {"rep": to // n_blk, "blk": lax.rem(to, n_blk)}

    def blk_peer(k):
        return {"blk": lax.rem(my_blk + k, n_blk)}

    def rep_peer(k):
        return {"rep": lax.rem(my_rep + k, n_rep)}

    def tp_peer(k):
        return {"tp": lax.rem(my_tp + k, n_tp)}

    barrier = pltpu.get_barrier_semaphore()
    each(1, n_all, lambda k: pl.semaphore_signal(
        barrier, inc=1, device_id=flat_peer(k), device_id_type=MESH))
    each(1, n_tp, lambda k: pl.semaphore_signal(
        barrier, inc=1, device_id=tp_peer(k), device_id_type=MESH))

    local = []

    def bring(src, dst):
        copy = pltpu.make_async_copy(src, dst, w_sem.at[len(local)])
        copy.start()
        local.append(copy)
        return copy

    def bring_layer(l, pieces):
        g = {}
        g["qkv"] = [bring(wqkv_hbm.at[l, j], wqkv.at[l, j]) for j in range(3)]
        step = n_ff // pieces
        g["fc1"] = [
            bring(wfc1_hbm.at[l, :, pl.ds(c * width, step * width)],
                  wfc1.at[l, :, pl.ds(c * width, step * width)])
            if c % step == 0 else None for c in range(n_ff)
        ]
        g["cache"] = [
            bring(cache_hbm.at[l, i], cache.at[l, i, pl.ds(0, slots)]) for i in range(2)]
        g["fc2"] = [
            bring(wfc2_hbm.at[l, pl.ds(i * ff_half * width, ff_half * width), :], wfc2.at[l, i])
            for i in range(2)
        ]
        g["out"] = [bring(wout_hbm.at[l], wout.at[l])]
        return g

    got = {0: bring_layer(0, n_ff // 2)}

    def remote(src, dst, ssem, rsem, peer):
        return pltpu.make_async_remote_copy(
            src_ref=src, dst_ref=dst, send_sem=ssem, recv_sem=rsem,
            device_id=peer, device_id_type=MESH)

    def copy_a(l, part):
        piece = pl.ds(2 * part, 2)
        return lambda k: remote(
            buf_a.at[l, 0, piece], buf_a.at[l, k, piece],
            a_send.at[l, k, part], a_recv.at[l, k, part], blk_peer(k))

    def copy_i(l):
        return lambda k: remote(
            buf_i.at[l, 0], buf_i.at[l, k], i_send.at[l, k], i_recv.at[l, k], blk_peer(k))

    def copy_q(l):
        return lambda k: remote(
            buf_q.at[l, 0], buf_q.at[l, k], q_send.at[l, k], q_recv.at[l, k], rep_peer(k))

    def copy_b(l):
        return lambda k: remote(
            msg.at[l, lax.rem(my_flat + k, n_all) // n_blk], buf_b.at[l, k],
            b_send.at[l, k], b_recv.at[l, k], flat_peer(k))

    def copy_c(l):
        return lambda k: remote(
            buf_c.at[l, 0], buf_c.at[l, k], c_send.at[l, k], c_recv.at[l, k], tp_peer(k))

    feature = lax.rem(lane_iota((2 * rows, width)), HD)
    small = (2 * rows, 128)
    posv = jnp.zeros(small, f32)
    for r in range(rows):
        posv = jnp.where(
            lax.rem(row_iota(small), rows) == r, pos_ref[r].astype(f32), posv)
    angles = posv * freq_ref[...]
    cosine = jnp.concatenate([jnp.cos(angles)] * (width // 128), axis=1)
    sine = jnp.concatenate([jnp.sin(angles)] * (width // 128), axis=1)
    sine = jnp.where(feature < ROT // 2, -sine, sine)

    extra = cache.shape[2] - slots
    columns = (slots + extra) * PAGE
    lanes = lane_iota((1, columns))
    col_owner = jnp.full((1, columns), -1, jnp.int32)
    home = jnp.full((slots, width), -1, jnp.int32)
    for s in range(slots):
        limit = jnp.where(used_ref[s] == 1, fill_ref[s], 0)
        here = (lanes >= s * PAGE) & (lanes < s * PAGE + limit)
        col_owner = jnp.where(here, owner_ref[s], col_owner)
        home_row = jnp.where(tail_ref[s] == 1, owner_ref[s] - my_rep * rows, -1)
        home = jnp.where(row_iota((slots, width)) == s, home_row, home)
        new_lane = jnp.where(tail_ref[s] == 1, slots * PAGE + home_row, -1)
        col_owner = jnp.where(lanes == new_lane, owner_ref[s], col_owner)
        write_pos = jnp.where(tail_ref[s] == 1, fill_ref[s], -1)
        bound_ref[s] = jnp.where(
            row_iota((PAGE, width)) == write_pos, -jnp.inf, jnp.inf).astype(bf16)
    mask_ref[...] = jnp.where(
        lax.rem(row_iota((heads * reqs, columns)), reqs) == col_owner, 1.0, 0.0)
    for l in range(LAYERS):
        for i in range(2):
            for s in range(slots, slots + extra):
                cache[l, i, s] = jnp.zeros((PAGE, width), bf16)

    head_of_lane = lane_iota((1, width)) // HD

    def expand(stat):
        out = jnp.broadcast_to(stat[:, 0:1], (stat.shape[0], width))
        for h in range(1, heads):
            out = jnp.where(head_of_lane == h, stat[:, h:h + 1], out)
        return out

    def fold(x):
        part = x.shape[1] // 4
        return jnp.concatenate([x[:, c * part:(c + 1) * part] for c in range(4)], axis=0)

    def unfold(x):
        x = x.astype(f32)
        return jnp.concatenate([x[c * rows:(c + 1) * rows] for c in range(4)], axis=1)

    def split(x):
        high = x.astype(bf16).astype(f32)
        return high, (x - high).astype(bf16).astype(f32)

    wide = model >= 512

    def fold_c(x):
        if wide:
            return fold(x)
        x = jnp.concatenate([x, jnp.zeros((16 - rows, model), f32)], axis=0)
        if model < buf_c.shape[3]:
            x = jnp.concatenate([x, jnp.zeros((16, buf_c.shape[3] - model), f32)], axis=1)
        return x

    def unfold_c(x):
        if wide:
            return unfold(x)
        return x[0:rows, 0:model]

    state = hidden_ref[...].astype(f32)
    for l in range(LAYERS):
        g = got[l]
        own_mean = jnp.sum(state, axis=1, keepdims=True) / model
        centered = state - own_mean
        own_square = jnp.sum(centered * centered, axis=1, keepdims=True)
        gain = gain_ref[l:l + 1, :]
        gain_hi = gain.astype(bf16).astype(f32)
        gain_lo = gain - gain_hi
        lhs = jnp.concatenate(
            [centered * gain, gain_hi, gain_lo, jnp.zeros((2 * rows - rows - 2, model), f32)],
            axis=0).astype(bf16)
        stat_lane = lane_iota((rows, width))
        stats = jnp.where(stat_lane < 128, own_mean, own_square)
        buf_a[l, 0, 0] = jnp.concatenate([stats, jnp.zeros((rows, width), f32)], axis=0)

        def project(j):
            g["qkv"][j].wait()
            buf_a[l, 0, 1 + j] = jnp.dot(lhs, wqkv[l, j], preferred_element_type=f32)

        def project_ff(c):
            if g["fc1"][c] is not None:
                g["fc1"][c].wait()
            buf_i[l, 0, c] = jnp.dot(
                lhs, wfc1[l, :, c * width:(c + 1) * width], preferred_element_type=f32)

        project(0)
        if l == 0:
            pl.semaphore_wait(barrier, n_all - 1 + n_tp - 1)
        each(1, n_blk, lambda k: copy_a(l, 0)(k).start())
        project(1)
        project(2)
        each(1, n_blk, lambda k: copy_a(l, 1)(k).start())
        for c in range(ff_half):
            project_ff(c)

        each(1, n_blk, lambda k: copy_a(l, 0)(k).wait_recv())
        mean = fold_sum(0, n_blk, lambda k, t: t + buf_a[l, k, 0, 0:rows, 0:1],
                        jnp.zeros((rows, 1), f32)) / n_blk

        def add_square(k, total):
            off = buf_a[l, k, 0, 0:rows, 0:1] - mean
            return total + (buf_a[l, k, 0, 0:rows, 128:129] + model * (off * off))

        square = fold_sum(0, n_blk, add_square, jnp.zeros((rows, 1), f32))
        scale = lax.rsqrt(square / full_model + EPSILON)

        def finish(buf, j):
            def add(k, total):
                off = buf_a[l, k, 0, 0:rows, 0:1] - mean
                block = buf[l, k, j]
                gained = block[rows:rows + 1] + block[rows + 1:rows + 2]
                return total + (block[0:rows] + off * gained)

            return fold_sum(0, n_blk, add, jnp.zeros((rows, width), f32)) * scale

        def rotate(x):
            turned = jnp.where(
                feature < ROT // 2,
                pltpu.roll(x, width - ROT // 2, 1),
                pltpu.roll(x, ROT // 2, 1))
            return (x * cosine + turned * sine).astype(bf16).astype(f32)

        blank = jnp.zeros((rows, width), f32)
        own_queries = rotate(jnp.concatenate([finish(buf_a, 1), blank], axis=0))[:rows]
        buf_q[l, 0] = fold(own_queries).astype(bf16)
        each(1, n_rep, lambda k: copy_q(l)(k).start())
        for c in range(ff_half, n_ff):
            project_ff(c)
        each(1, n_blk, lambda k: copy_i(l)(k).start())
        if l + 1 < LAYERS:
            got[l + 1] = bring_layer(l + 1, 1)
        each(1, n_blk, lambda k: copy_a(l, 1)(k).wait_recv())
        new_k = rotate(jnp.concatenate([finish(buf_a, 2), blank], axis=0))[:rows]
        new_v = finish(buf_a, 3).astype(bf16).astype(f32)
        new = (new_k, new_v)
        for i in range(2):
            cache[l, i, slots, 0:16] = jnp.concatenate(
                [new[i], jnp.zeros((16 - rows, width), f32)], axis=0).astype(bf16)

        each(1, n_blk, lambda k: copy_i(l)(k).wait_recv())
        for c in range(n_ff):
            act = jax.nn.gelu(finish(buf_i, c), approximate=True)
            act_ref[c] = jnp.concatenate([act, jnp.zeros((rows, width), f32)], axis=0).astype(bf16)
        g["fc2"][0].wait()
        mlp_acc[...] = jnp.dot(
            jnp.concatenate([act_ref[c] for c in range(ff_half)], axis=1),
            wfc2[l, 0], preferred_element_type=f32)

        each(1, n_rep, lambda k: copy_q(l)(k).wait_recv())
        queries = jnp.concatenate(
            [unfold(buf_q[l, lax.rem(my_rep - t + n_rep, n_rep)]) for t in range(n_rep)], axis=0)
        by_head = jnp.concatenate(
            [jnp.where(head_of_lane == h, queries, 0.0) for h in range(heads)], axis=0
        ).astype(bf16)
        for i in range(2):
            g["cache"][i].wait()
        keys = cache[l, 0].reshape(columns, width)
        values = cache[l, 1].reshape(columns, width)
        scores = lax.dot_general(
            by_head, keys, (((1,), (1,)), ((), ())), preferred_element_type=f32) * HD ** (-0.5)
        mask = mask_ref[...] > 0.0
        scores = jnp.where(mask, scores, LOWEST)
        high_pieces = split(jnp.max(scores, axis=1, keepdims=True))
        highest = high_pieces[0] + high_pieces[1]
        weights = jnp.where(mask, jnp.exp(scores - highest), 0.0)
        totals = jnp.sum(weights, axis=1, keepdims=True)
        spread = jnp.dot(weights.astype(bf16), values, preferred_element_type=f32)
        out = spread[0:reqs]
        stat_shape = (reqs, 128)
        stats = [jnp.zeros(stat_shape, f32), jnp.zeros(stat_shape, f32),
                 jnp.ones(stat_shape, f32), jnp.zeros(stat_shape, f32)]
        for h in range(heads):
            part = slice(h * reqs, (h + 1) * reqs)
            if h > 0:
                out = jnp.where(head_of_lane == h, spread[part], out)
            for i, piece in enumerate(high_pieces + split(totals)):
                stats[i] = jnp.where(lane_iota(stat_shape) == h, piece[part], stats[i])
        for r in range(n_rep):
            part = slice(r * rows, (r + 1) * rows)
            msg[l, r] = jnp.concatenate(
                [fold(out[part]), jnp.concatenate([stat[part] for stat in stats], axis=0)],
                axis=1).astype(bf16)
        each(1, n_all, lambda k: copy_b(l)(k).start())
        buf_b[l, 0] = msg[l, my_rep]

        g["fc2"][1].wait()
        mlp_acc[...] += jnp.dot(
            jnp.concatenate([act_ref[c] for c in range(ff_half, n_ff)], axis=1),
            wfc2[l, 1], preferred_element_type=f32)

        each(1, n_all, lambda k: copy_b(l)(k).wait_recv())

        def stat_of(k, first):
            stat = buf_b[l, k, :, quarter:quarter + 128].astype(f32)
            return stat[first * rows:(first + 1) * rows] + stat[(first + 1) * rows:(first + 2) * rows]

        top = fold_sum(
            0, n_all, lambda k, t: jnp.maximum(t, stat_of(k, 0)),
            jnp.full((rows, 128), LOWEST, f32))

        def merge(k, carry):
            denom, numer = carry
            factor = jnp.exp(stat_of(k, 0) - top)
            denom = denom + factor * stat_of(k, 2)
            numer = numer + expand(factor) * unfold(buf_b[l, k, :, 0:quarter])
            return denom, numer

        denom, numer = fold_sum(
            0, n_all, merge, (jnp.zeros((rows, 128), f32), jnp.zeros((rows, width), f32)))
        attended = numer / expand(denom)
        attended = jnp.concatenate(
            [attended, jnp.zeros((rows, width), f32)], axis=0).astype(bf16)
        g["out"][0].wait()
        branch = (
            jnp.dot(attended, wout[l], preferred_element_type=f32) + mlp_acc[...])[0:rows]
        buf_c[l, 0] = fold_c(branch).astype(bf16)
        each(1, n_tp, lambda k: copy_c(l)(k).start())

        for i in range(2):
            fresh = jnp.zeros((slots, width), f32)
            for r in range(rows):
                fresh = jnp.where(home == r, new[i][r:r + 1], fresh)
            fresh_ref[l, i] = fresh.astype(bf16)

        each(1, n_blk, lambda k: copy_a(l, 0)(k).wait_send())
        each(1, n_blk, lambda k: copy_a(l, 1)(k).wait_send())
        each(1, n_blk, lambda k: copy_i(l)(k).wait_send())
        each(1, n_rep, lambda k: copy_q(l)(k).wait_send())
        each(1, n_all, lambda k: copy_b(l)(k).wait_send())

        each(1, n_tp, lambda k: copy_c(l)(k).wait_recv())
        total = buf_c[l, lax.rem(my_tp + n_tp, n_tp)].astype(f32)
        for t in range(1, n_tp):
            total = total + buf_c[l, lax.rem(my_tp - t + n_tp, n_tp)].astype(f32)
        total = unfold_c(total)
        state = (state + total).astype(bf16).astype(f32)

    state_ref[...] = state
    for l in range(LAYERS):
        each(1, n_tp, lambda k: copy_c(l)(k).wait_send())


def frequencies(rows):
    feature = np.arange(128) % HD
    power = 10000.0 ** (-2.0 * (feature % (ROT // 2)) / ROT)
    return np.tile(np.where(feature < ROT, power, 0.0).astype(np.float32)[None, :], (rows, 1))


def per_device(
    hidden, ln_gain, w_qkv, w_fc1, w_out, w_fc2, caches,
    page_owner, page_used, page_fill, page_tail, positions,
):
    n_rep, n_blk, n_tp = (lax.axis_size(a) for a in ("rep", "blk", "tp"))
    f32, bf16 = jnp.float32, jnp.bfloat16
    rows, model = hidden.shape
    slots = page_owner.shape[0]
    width = w_out.shape[1]
    n_ff = w_fc1.shape[2] // width
    n_all = n_rep * n_blk
    wq = jnp.transpose(w_qkv, (0, 2, 1, 3))
    c_width = model // 4 if model >= 512 else max(model, 128)
    extra = 128 // PAGE
    smem = pl.BlockSpec(memory_space=pltpu.SMEM)
    vmem = pl.BlockSpec(memory_space=pltpu.VMEM)
    anywhere = pl.BlockSpec(memory_space=pl.ANY)
    dma = pltpu.SemaphoreType.DMA
    n_copies = LAYERS * (3 + n_ff + 2 + 2 + 1)
    state, fresh, bound = pl.pallas_call(
        functools.partial(kernel, n_rep, n_blk, n_tp),
        out_shape=(
            pltpu.VMEM((rows, model), f32),
            pltpu.VMEM((LAYERS, 2, slots, width), bf16),
            pltpu.VMEM((slots, PAGE, width), bf16),
        ),
        in_specs=[smem] * 5 + [vmem] * 3 + [anywhere] * 5,
        out_specs=(vmem, vmem, vmem),
        scratch_shapes=[
            pltpu.VMEM((LAYERS, 3, model, width), bf16),
            pltpu.VMEM((LAYERS, model, n_ff * width), bf16),
            pltpu.VMEM((LAYERS, width, model), bf16),
            pltpu.VMEM((LAYERS, 2, n_ff // 2 * width, model), bf16),
            pltpu.VMEM((LAYERS, 2, slots + extra, PAGE, width), bf16),
            pltpu.VMEM((LAYERS, n_blk, 4, 2 * rows, width), f32),
            pltpu.VMEM((LAYERS, n_blk, n_ff, 2 * rows, width), f32),
            pltpu.VMEM((LAYERS, n_rep, 4 * rows, width // 4), bf16),
            pltpu.VMEM((LAYERS, n_rep, 4 * rows, width // 4 + 128), bf16),
            pltpu.VMEM((LAYERS, n_all, 4 * rows, width // 4 + 128), bf16),
            pltpu.VMEM((LAYERS, n_tp, 16, c_width), bf16),
            pltpu.VMEM((2 * rows, model), f32),
            pltpu.VMEM((n_ff, 2 * rows, width), bf16),
            pltpu.VMEM((width // HD * rows * n_rep, (slots + extra) * PAGE), f32),
            dma((n_copies,)),
            dma((LAYERS, n_blk, 2)), dma((LAYERS, n_blk, 2)),
            dma((LAYERS, n_blk)), dma((LAYERS, n_blk)),
            dma((LAYERS, n_rep)), dma((LAYERS, n_rep)),
            dma((LAYERS, n_all)), dma((LAYERS, n_all)),
            dma((LAYERS, n_tp)), dma((LAYERS, n_tp)),
        ],
        compiler_params=pltpu.CompilerParams(
            collective_id=0, has_side_effects=True, vmem_limit_bytes=57 * 2**20),
        name="decode_layers",
    )(
        page_owner, page_used, page_fill, page_tail, positions,
        hidden, ln_gain, jnp.asarray(frequencies(2 * rows)),
        wq, w_fc1, w_out, w_fc2, caches,
    )
    caches_out = jnp.where(caches < bound[None, None], caches, fresh[:, :, :, None, :])
    return (state.astype(bf16), caches_out)


def solution(mesh):
    in_specs = (
        P("rep", "blk"),
        P(None, "blk"),
        P(None, "blk", None, "tp"),
        P(None, "blk", "tp"),
        P(None, "tp", "blk"),
        P(None, "tp", "blk"),
        P(None, None, ("rep", "blk"), None, "tp"),
        P(("rep", "blk")),
        P(("rep", "blk")),
        P(("rep", "blk")),
        P(("rep", "blk")),
        P("rep"),
    )
    out_specs = (P("rep", "blk"), P(None, None, ("rep", "blk"), None, "tp"))
    return jax.shard_map(
        per_device, mesh=mesh, in_specs=in_specs, out_specs=out_specs, check_vma=False
    )
```

```python
import functools

import jax
import jax.numpy as jnp
import numpy as np
from jax import lax
from jax.experimental import pallas as pl
from jax.experimental.pallas import tpu as pltpu
from jax.sharding import PartitionSpec as P

HD = 64
ROT = 32
LAYERS = 2
PAGE = 32
EPSILON = 1e-05
LOWEST = -1e30
MESH = pl.DeviceIdType.MESH
UNROLL = 8


def each(start, stop, body):
    if stop - start <= UNROLL:
        for k in range(start, stop):
            body(k)
    else:
        lax.fori_loop(start, stop, lambda k, c: (body(k), c)[1], 0)


def fold_sum(start, stop, body, carry):
    if stop - start <= UNROLL:
        for k in range(start, stop):
            carry = body(k, carry)
        return carry
    return lax.fori_loop(start, stop, body, carry)


def lane_iota(shape):
    return lax.broadcasted_iota(jnp.int32, shape, len(shape) - 1)


def row_iota(shape):
    return lax.broadcasted_iota(jnp.int32, shape, len(shape) - 2)


def kernel(
    n_rep, n_blk, n_tp,
    owner_ref, used_ref, fill_ref, tail_ref, pos_ref,
    hidden_ref, gain_ref, freq_ref,
    wqkv_hbm, wfc1_hbm, wout_hbm, wfc2_hbm, cache_hbm,
    state_ref, fresh_ref, bound_ref,
    wqkv, wfc1, wout, wfc2, cache,
    buf_a, buf_i, buf_q, msg, buf_b, buf_c, mlp_acc, act_ref, mask_ref,
    w_sem, a_send, a_recv, i_send, i_recv, q_send, q_recv, b_send, b_recv, c_send, c_recv,
):
    f32, bf16 = jnp.float32, jnp.bfloat16
    rows, model = hidden_ref.shape
    full_model = model * n_blk
    slots = owner_ref.shape[0]
    width = wout.shape[1]
    heads = width // HD
    n_ff = wfc1.shape[2] // width
    reqs = rows * n_rep
    n_all = n_rep * n_blk
    quarter = width // 4
    my_rep, my_blk, my_tp = lax.axis_index("rep"), lax.axis_index("blk"), lax.axis_index("tp")
    my_flat = my_rep * n_blk + my_blk
    ff_half = n_ff // 2

    def flat_peer(k):
        to = lax.rem(my_flat + k, n_all)
        return {"rep": to // n_blk, "blk": lax.rem(to, n_blk)}

    def blk_peer(k):
        return {"blk": lax.rem(my_blk + k, n_blk)}

    def rep_peer(k):
        return {"rep": lax.rem(my_rep + k, n_rep)}

    def tp_peer(k):
        return {"tp": lax.rem(my_tp + k, n_tp)}

    barrier = pltpu.get_barrier_semaphore()
    each(1, n_all, lambda k: pl.semaphore_signal(
        barrier, inc=1, device_id=flat_peer(k), device_id_type=MESH))
    each(1, n_tp, lambda k: pl.semaphore_signal(
        barrier, inc=1, device_id=tp_peer(k), device_id_type=MESH))

    local = []

    def bring(src, dst):
        copy = pltpu.make_async_copy(src, dst, w_sem.at[len(local)])
        copy.start()
        local.append(copy)
        return copy

    def bring_layer(l, pieces):
        g = {}
        g["qkv"] = [bring(wqkv_hbm.at[l, j], wqkv.at[l, j]) for j in range(3)]
        step = n_ff // pieces
        g["fc1"] = [
            bring(wfc1_hbm.at[l, :, pl.ds(c * width, step * width)],
                  wfc1.at[l, :, pl.ds(c * width, step * width)])
            if c % step == 0 else None for c in range(n_ff)
        ]
        g["cache"] = [
            bring(cache_hbm.at[l, i], cache.at[l, i, pl.ds(0, slots)]) for i in range(2)]
        g["fc2"] = [
            bring(wfc2_hbm.at[l, pl.ds(i * ff_half * width, ff_half * width), :], wfc2.at[l, i])
            for i in range(2)
        ]
        g["out"] = [bring(wout_hbm.at[l], wout.at[l])]
        return g

    got = {0: bring_layer(0, n_ff // 2)}

    def remote(src, dst, ssem, rsem, peer):
        return pltpu.make_async_remote_copy(
            src_ref=src, dst_ref=dst, send_sem=ssem, recv_sem=rsem,
            device_id=peer, device_id_type=MESH)

    def copy_a(l, part):
        piece = pl.ds(2 * part, 2)
        return lambda k: remote(
            buf_a.at[l, 0, piece], buf_a.at[l, k, piece],
            a_send.at[l, k, part], a_recv.at[l, k, part], blk_peer(k))

    def copy_i(l):
        return lambda k: remote(
            buf_i.at[l, 0], buf_i.at[l, k], i_send.at[l, k], i_recv.at[l, k], blk_peer(k))

    def copy_q(l):
        return lambda k: remote(
            buf_q.at[l, 0], buf_q.at[l, k], q_send.at[l, k], q_recv.at[l, k], rep_peer(k))

    def copy_b(l):
        return lambda k: remote(
            msg.at[l, lax.rem(my_flat + k, n_all) // n_blk], buf_b.at[l, k],
            b_send.at[l, k], b_recv.at[l, k], flat_peer(k))

    def copy_c(l):
        return lambda k: remote(
            buf_c.at[l, 0], buf_c.at[l, k], c_send.at[l, k], c_recv.at[l, k], tp_peer(k))

    feature = lax.rem(lane_iota((2 * rows, width)), HD)
    small = (2 * rows, 128)
    posv = jnp.zeros(small, f32)
    for r in range(rows):
        posv = jnp.where(
            lax.rem(row_iota(small), rows) == r, pos_ref[r].astype(f32), posv)
    angles = posv * freq_ref[...]
    cosine = jnp.concatenate([jnp.cos(angles)] * (width // 128), axis=1)
    sine = jnp.concatenate([jnp.sin(angles)] * (width // 128), axis=1)
    sine = jnp.where(feature < ROT // 2, -sine, sine)

    extra = cache.shape[2] - slots
    columns = (slots + extra) * PAGE
    lanes = lane_iota((1, columns))
    col_owner = jnp.full((1, columns), -1, jnp.int32)
    home = jnp.full((slots, width), -1, jnp.int32)
    for s in range(slots):
        limit = jnp.where(used_ref[s] == 1, fill_ref[s], 0)
        here = (lanes >= s * PAGE) & (lanes < s * PAGE + limit)
        col_owner = jnp.where(here, owner_ref[s], col_owner)
        home_row = jnp.where(tail_ref[s] == 1, owner_ref[s] - my_rep * rows, -1)
        home = jnp.where(row_iota((slots, width)) == s, home_row, home)
        new_lane = jnp.where(tail_ref[s] == 1, slots * PAGE + home_row, -1)
        col_owner = jnp.where(lanes == new_lane, owner_ref[s], col_owner)
        write_pos = jnp.where(tail_ref[s] == 1, fill_ref[s], -1)
        bound_ref[s] = jnp.where(
            row_iota((PAGE, width)) == write_pos, -jnp.inf, jnp.inf).astype(bf16)
    mask_ref[...] = jnp.where(
        lax.rem(row_iota((heads * reqs, columns)), reqs) == col_owner, 1.0, 0.0)
    for l in range(LAYERS):
        for i in range(2):
            for s in range(slots, slots + extra):
                cache[l, i, s] = jnp.zeros((PAGE, width), bf16)

    head_of_lane = lane_iota((1, width)) // HD

    def expand(stat):
        out = jnp.broadcast_to(stat[:, 0:1], (stat.shape[0], width))
        for h in range(1, heads):
            out = jnp.where(head_of_lane == h, stat[:, h:h + 1], out)
        return out

    def fold(x):
        part = x.shape[1] // 4
        return jnp.concatenate([x[:, c * part:(c + 1) * part] for c in range(4)], axis=0)

    def unfold(x):
        x = x.astype(f32)
        return jnp.concatenate([x[c * rows:(c + 1) * rows] for c in range(4)], axis=1)

    def split(x):
        high = x.astype(bf16).astype(f32)
        return high, (x - high).astype(bf16).astype(f32)

    wide = model >= 512

    def fold_c(x):
        if wide:
            return fold(x)
        x = jnp.concatenate([x, jnp.zeros((16 - rows, model), f32)], axis=0)
        if model < buf_c.shape[3]:
            x = jnp.concatenate([x, jnp.zeros((16, buf_c.shape[3] - model), f32)], axis=1)
        return x

    def unfold_c(x):
        if wide:
            return unfold(x)
        return x[0:rows, 0:model]

    state = hidden_ref[...].astype(f32)
    for l in range(LAYERS):
        g = got[l]
        own_mean = jnp.sum(state, axis=1, keepdims=True) / model
        centered = state - own_mean
        own_square = jnp.sum(centered * centered, axis=1, keepdims=True)
        gain = gain_ref[l:l + 1, :]
        gain_hi = gain.astype(bf16).astype(f32)
        gain_lo = gain - gain_hi
        lhs = jnp.concatenate(
            [centered * gain, gain_hi, gain_lo, jnp.zeros((2 * rows - rows - 2, model), f32)],
            axis=0).astype(bf16)
        stat_lane = lane_iota((rows, width))
        stats = jnp.where(stat_lane < 128, own_mean, own_square)
        buf_a[l, 0, 0] = jnp.concatenate([stats, jnp.zeros((rows, width), f32)], axis=0)

        def project(j):
            g["qkv"][j].wait()
            buf_a[l, 0, 1 + j] = jnp.dot(lhs, wqkv[l, j], preferred_element_type=f32)

        def project_ff(c):
            if g["fc1"][c] is not None:
                g["fc1"][c].wait()
            buf_i[l, 0, c] = jnp.dot(
                lhs, wfc1[l, :, c * width:(c + 1) * width], preferred_element_type=f32)

        project(0)
        if l == 0:
            pl.semaphore_wait(barrier, n_all - 1 + n_tp - 1)
        each(1, n_blk, lambda k: copy_a(l, 0)(k).start())
        project(1)
        project(2)
        each(1, n_blk, lambda k: copy_a(l, 1)(k).start())
        for c in range(ff_half):
            project_ff(c)

        each(1, n_blk, lambda k: copy_a(l, 0)(k).wait_recv())
        mean = fold_sum(0, n_blk, lambda k, t: t + buf_a[l, k, 0, 0:rows, 0:1],
                        jnp.zeros((rows, 1), f32)) / n_blk

        def add_square(k, total):
            off = buf_a[l, k, 0, 0:rows, 0:1] - mean
            return total + (buf_a[l, k, 0, 0:rows, 128:129] + model * (off * off))

        square = fold_sum(0, n_blk, add_square, jnp.zeros((rows, 1), f32))
        scale = lax.rsqrt(square / full_model + EPSILON)

        def finish(buf, j):
            def add(k, total):
                off = buf_a[l, k, 0, 0:rows, 0:1] - mean
                block = buf[l, k, j]
                gained = block[rows:rows + 1] + block[rows + 1:rows + 2]
                return total + (block[0:rows] + off * gained)

            return fold_sum(0, n_blk, add, jnp.zeros((rows, width), f32)) * scale

        def rotate(x):
            turned = jnp.where(
                feature < ROT // 2,
                pltpu.roll(x, width - ROT // 2, 1),
                pltpu.roll(x, ROT // 2, 1))
            return (x * cosine + turned * sine).astype(bf16).astype(f32)

        blank = jnp.zeros((rows, width), f32)
        own_queries = rotate(jnp.concatenate([finish(buf_a, 1), blank], axis=0))[:rows]
        buf_q[l, 0] = fold(own_queries).astype(bf16)
        each(1, n_rep, lambda k: copy_q(l)(k).start())
        for c in range(ff_half, n_ff):
            project_ff(c)
        each(1, n_blk, lambda k: copy_i(l)(k).start())
        each(1, n_blk, lambda k: copy_a(l, 1)(k).wait_recv())
        new_k = rotate(jnp.concatenate([finish(buf_a, 2), blank], axis=0))[:rows]
        new_v = finish(buf_a, 3).astype(bf16).astype(f32)
        new = (new_k, new_v)
        for i in range(2):
            cache[l, i, slots, 0:16] = jnp.concatenate(
                [new[i], jnp.zeros((16 - rows, width), f32)], axis=0).astype(bf16)

        each(1, n_blk, lambda k: copy_i(l)(k).wait_recv())
        for c in range(n_ff):
            act = jax.nn.gelu(finish(buf_i, c), approximate=True)
            act_ref[c] = jnp.concatenate([act, jnp.zeros((rows, width), f32)], axis=0).astype(bf16)
        g["fc2"][0].wait()
        mlp_acc[...] = jnp.dot(
            jnp.concatenate([act_ref[c] for c in range(ff_half)], axis=1),
            wfc2[l, 0], preferred_element_type=f32)

        each(1, n_rep, lambda k: copy_q(l)(k).wait_recv())
        queries = jnp.concatenate(
            [unfold(buf_q[l, lax.rem(my_rep - t + n_rep, n_rep)]) for t in range(n_rep)], axis=0)
        by_head = jnp.concatenate(
            [jnp.where(head_of_lane == h, queries, 0.0) for h in range(heads)], axis=0
        ).astype(bf16)
        for i in range(2):
            g["cache"][i].wait()
        keys = cache[l, 0].reshape(columns, width)
        values = cache[l, 1].reshape(columns, width)
        scores = lax.dot_general(
            by_head, keys, (((1,), (1,)), ((), ())), preferred_element_type=f32) * HD ** (-0.5)
        mask = mask_ref[...] > 0.0
        scores = jnp.where(mask, scores, LOWEST)
        high_pieces = split(jnp.max(scores, axis=1, keepdims=True))
        highest = high_pieces[0] + high_pieces[1]
        weights = jnp.where(mask, jnp.exp(scores - highest), 0.0)
        totals = jnp.sum(weights, axis=1, keepdims=True)
        spread = jnp.dot(weights.astype(bf16), values, preferred_element_type=f32)
        out = spread[0:reqs]
        stat_shape = (reqs, 128)
        stats = [jnp.zeros(stat_shape, f32), jnp.zeros(stat_shape, f32),
                 jnp.ones(stat_shape, f32), jnp.zeros(stat_shape, f32)]
        for h in range(heads):
            part = slice(h * reqs, (h + 1) * reqs)
            if h > 0:
                out = jnp.where(head_of_lane == h, spread[part], out)
            for i, piece in enumerate(high_pieces + split(totals)):
                stats[i] = jnp.where(lane_iota(stat_shape) == h, piece[part], stats[i])
        for r in range(n_rep):
            part = slice(r * rows, (r + 1) * rows)
            msg[l, r] = jnp.concatenate(
                [fold(out[part]), jnp.concatenate([stat[part] for stat in stats], axis=0)],
                axis=1).astype(bf16)
        each(1, n_all, lambda k: copy_b(l)(k).start())
        if l + 1 < LAYERS:
            got[l + 1] = bring_layer(l + 1, 1)
        buf_b[l, 0] = msg[l, my_rep]

        g["fc2"][1].wait()
        mlp_acc[...] += jnp.dot(
            jnp.concatenate([act_ref[c] for c in range(ff_half, n_ff)], axis=1),
            wfc2[l, 1], preferred_element_type=f32)

        each(1, n_all, lambda k: copy_b(l)(k).wait_recv())

        def stat_of(k, first):
            stat = buf_b[l, k, :, quarter:quarter + 128].astype(f32)
            return stat[first * rows:(first + 1) * rows] + stat[(first + 1) * rows:(first + 2) * rows]

        top = fold_sum(
            0, n_all, lambda k, t: jnp.maximum(t, stat_of(k, 0)),
            jnp.full((rows, 128), LOWEST, f32))

        def merge(k, carry):
            denom, numer = carry
            factor = jnp.exp(stat_of(k, 0) - top)
            denom = denom + factor * stat_of(k, 2)
            numer = numer + expand(factor) * unfold(buf_b[l, k, :, 0:quarter])
            return denom, numer

        denom, numer = fold_sum(
            0, n_all, merge, (jnp.zeros((rows, 128), f32), jnp.zeros((rows, width), f32)))
        attended = numer / expand(denom)
        attended = jnp.concatenate(
            [attended, jnp.zeros((rows, width), f32)], axis=0).astype(bf16)
        g["out"][0].wait()
        branch = (
            jnp.dot(attended, wout[l], preferred_element_type=f32) + mlp_acc[...])[0:rows]
        buf_c[l, 0] = fold_c(branch).astype(bf16)
        each(1, n_tp, lambda k: copy_c(l)(k).start())

        for i in range(2):
            fresh = jnp.zeros((slots, width), f32)
            for r in range(rows):
                fresh = jnp.where(home == r, new[i][r:r + 1], fresh)
            fresh_ref[l, i] = fresh.astype(bf16)

        each(1, n_blk, lambda k: copy_a(l, 0)(k).wait_send())
        each(1, n_blk, lambda k: copy_a(l, 1)(k).wait_send())
        each(1, n_blk, lambda k: copy_i(l)(k).wait_send())
        each(1, n_rep, lambda k: copy_q(l)(k).wait_send())
        each(1, n_all, lambda k: copy_b(l)(k).wait_send())

        each(1, n_tp, lambda k: copy_c(l)(k).wait_recv())
        total = buf_c[l, lax.rem(my_tp + n_tp, n_tp)].astype(f32)
        for t in range(1, n_tp):
            total = total + buf_c[l, lax.rem(my_tp - t + n_tp, n_tp)].astype(f32)
        total = unfold_c(total)
        state = (state + total).astype(bf16).astype(f32)

    state_ref[...] = state
    for l in range(LAYERS):
        each(1, n_tp, lambda k: copy_c(l)(k).wait_send())


def frequencies(rows):
    feature = np.arange(128) % HD
    power = 10000.0 ** (-2.0 * (feature % (ROT // 2)) / ROT)
    return np.tile(np.where(feature < ROT, power, 0.0).astype(np.float32)[None, :], (rows, 1))


def per_device(
    hidden, ln_gain, w_qkv, w_fc1, w_out, w_fc2, caches,
    page_owner, page_used, page_fill, page_tail, positions,
):
    n_rep, n_blk, n_tp = (lax.axis_size(a) for a in ("rep", "blk", "tp"))
    f32, bf16 = jnp.float32, jnp.bfloat16
    rows, model = hidden.shape
    slots = page_owner.shape[0]
    width = w_out.shape[1]
    n_ff = w_fc1.shape[2] // width
    n_all = n_rep * n_blk
    wq = jnp.transpose(w_qkv, (0, 2, 1, 3))
    c_width = model // 4 if model >= 512 else max(model, 128)
    extra = 128 // PAGE
    smem = pl.BlockSpec(memory_space=pltpu.SMEM)
    vmem = pl.BlockSpec(memory_space=pltpu.VMEM)
    anywhere = pl.BlockSpec(memory_space=pl.ANY)
    dma = pltpu.SemaphoreType.DMA
    n_copies = LAYERS * (3 + n_ff + 2 + 2 + 1)
    state, fresh, bound = pl.pallas_call(
        functools.partial(kernel, n_rep, n_blk, n_tp),
        out_shape=(
            pltpu.VMEM((rows, model), f32),
            pltpu.VMEM((LAYERS, 2, slots, width), bf16),
            pltpu.VMEM((slots, PAGE, width), bf16),
        ),
        in_specs=[smem] * 5 + [vmem] * 3 + [anywhere] * 5,
        out_specs=(vmem, vmem, vmem),
        scratch_shapes=[
            pltpu.VMEM((LAYERS, 3, model, width), bf16),
            pltpu.VMEM((LAYERS, model, n_ff * width), bf16),
            pltpu.VMEM((LAYERS, width, model), bf16),
            pltpu.VMEM((LAYERS, 2, n_ff // 2 * width, model), bf16),
            pltpu.VMEM((LAYERS, 2, slots + extra, PAGE, width), bf16),
            pltpu.VMEM((LAYERS, n_blk, 4, 2 * rows, width), f32),
            pltpu.VMEM((LAYERS, n_blk, n_ff, 2 * rows, width), f32),
            pltpu.VMEM((LAYERS, n_rep, 4 * rows, width // 4), bf16),
            pltpu.VMEM((LAYERS, n_rep, 4 * rows, width // 4 + 128), bf16),
            pltpu.VMEM((LAYERS, n_all, 4 * rows, width // 4 + 128), bf16),
            pltpu.VMEM((LAYERS, n_tp, 16, c_width), bf16),
            pltpu.VMEM((2 * rows, model), f32),
            pltpu.VMEM((n_ff, 2 * rows, width), bf16),
            pltpu.VMEM((width // HD * rows * n_rep, (slots + extra) * PAGE), f32),
            dma((n_copies,)),
            dma((LAYERS, n_blk, 2)), dma((LAYERS, n_blk, 2)),
            dma((LAYERS, n_blk)), dma((LAYERS, n_blk)),
            dma((LAYERS, n_rep)), dma((LAYERS, n_rep)),
            dma((LAYERS, n_all)), dma((LAYERS, n_all)),
            dma((LAYERS, n_tp)), dma((LAYERS, n_tp)),
        ],
        compiler_params=pltpu.CompilerParams(
            collective_id=0, has_side_effects=True, vmem_limit_bytes=57 * 2**20),
        name="decode_layers",
    )(
        page_owner, page_used, page_fill, page_tail, positions,
        hidden, ln_gain, jnp.asarray(frequencies(2 * rows)),
        wq, w_fc1, w_out, w_fc2, caches,
    )
    caches_out = jnp.where(caches < bound[None, None], caches, fresh[:, :, :, None, :])
    return (state.astype(bf16), caches_out)


def solution(mesh):
    in_specs = (
        P("rep", "blk"),
        P(None, "blk"),
        P(None, "blk", None, "tp"),
        P(None, "blk", "tp"),
        P(None, "tp", "blk"),
        P(None, "tp", "blk"),
        P(None, None, ("rep", "blk"), None, "tp"),
        P(("rep", "blk")),
        P(("rep", "blk")),
        P(("rep", "blk")),
        P(("rep", "blk")),
        P("rep"),
    )
    out_specs = (P("rep", "blk"), P(None, None, ("rep", "blk"), None, "tp"))
    return jax.shard_map(
        per_device, mesh=mesh, in_specs=in_specs, out_specs=out_specs, check_vma=False
    )
```
